128 devices in a mesh: tm: 32 (over y, z, core), feat: 4 (over x).
Axes of the slice: x: 4, y: 4, z: 4, core: 2. Of those that a mesh axis runs over, the one named last changes fastest.
Arguments:
- snapshots: bfloat16 [8192, 512], P('tm'), may hold values from -6 to 6
- projection: bfloat16 [4096, 8192], P(None, 'feat'), may hold values from -0.09375 to 0.09375
- phase_shift: float32 [8192], P('feat'), may hold values from -3.140625 to 3.140625
Outputs:
- gram: float32 [8192, 2048], P('feat', 'tm')
- cross: float32 [8192, 2048], P('feat', 'tm')
The draws below stay inside these ranges and needn't reach their ends.
All inputs are finite; a program needn't handle non-finite values.
Results may differ from the reference program's by a relative error of at most 0.0003.
Values may be sent and summed in bfloat16 or wider, within the bound.
No kernel may reach another device: no remote copies, remote signals or barrier semaphores. Data moves between devices by JAX's collectives and lax.ppermute only.
A program may use at most 128 MiB of HBM per device.

```python
import math
import jax
import jax.numpy as jnp
from jax import lax

P_SIZE = 512
LAGS = 8
F = 8192
CWD = 512
TS = 8192
CW = 2048
N_FEAT = 4


def steps_of(stream_key, shape, split, low, largest):
    gain, own = 1.0, jax.random.fold_in(stream_key, 6)
    for axis_at, parts in split:
        heights = jnp.exp(jax.random.uniform(jax.random.fold_in(own, axis_at), (parts,), jnp.float32, low / len(split), largest / len(split)))
        gain = gain * jnp.repeat(heights, shape[axis_at] // parts).reshape([-1 if axis == axis_at else 1 for axis in range(len(shape))])
    return gain


def noise(own_key, extent, width, most, cuts=(), kind=jnp.bfloat16):
    result = jax.random.normal(own_key, extent, jnp.float32) * width
    if len(cuts) > 0:
        result = steps_of(own_key, extent, cuts, -0.22, 0.18) * result
    return jnp.clip(result, min=-most, max=most).astype(kind)


def setup_inputs(seed: int = 0) -> dict:
    streams_of = jax.random.split(jax.random.key(seed), 4)
    return {
        "snapshots": noise(streams_of[0], (TS, P_SIZE), 1.0, 6.0, ((0, 32),)),
        "projection": noise(streams_of[1], (LAGS * P_SIZE, F), (LAGS * P_SIZE) ** -0.5, 0.09375, ((1, 4),)),
        "phase_shift": jnp.clip(jax.random.uniform(streams_of[2], (F,), jnp.float32, -3.140625, 3.140625), -3.140625, 3.140625),
    }


root_two = math.sqrt(2.0)

def reference(snapshots, projection, phase_shift):
    zero_rows = jnp.zeros((LAGS - 1, P_SIZE), snapshots.dtype)
    padded = jnp.concatenate([zero_rows, snapshots], 0)
    embedded = jnp.concatenate([padded[LAGS - 1 - k:LAGS - 1 - k + TS] for k in range(LAGS)], 1)
    projected = jnp.dot(embedded, projection, preferred_element_type=jnp.float32) + phase_shift
    feats = root_two * jnp.cos(projected)
    shard_cols = F // N_FEAT
    window = feats.reshape(TS, N_FEAT, shard_cols)[:, :, :CWD].reshape(TS, CW)
    gram = lax.dot_general(feats, window, (((0,), (0,)), ((), ())), precision=lax.Precision.HIGHEST, preferred_element_type=jnp.float32) / TS
    cross = lax.dot_general(feats[:-1], window[1:], (((0,), (0,)), ((), ())), precision=lax.Precision.HIGHEST, preferred_element_type=jnp.float32) / (TS - 1)
    return (gram, cross)
```

```python
import math

import jax
import jax.numpy as jnp
import numpy as np
from jax import lax
from jax.sharding import PartitionSpec as P

CWD = 512
Y, Z, C = 4, 4, 2
HALO = 8

TWO_PI_HIGH = 6.28125
TWO_PI_LOW = 2 * math.pi - TWO_PI_HIGH


def half_cos_terms():
    fit = np.polynomial.chebyshev.Chebyshev.interpolate(
        lambda q: np.cos(np.sqrt(q) / 2), 4, domain=[0.0, (math.pi * 1.0005) ** 2]
    )
    return [float(v * math.sqrt(2 * math.sqrt(2.0))) for v in fit.convert(kind=np.polynomial.Polynomial).coef]


TERMS = half_cos_terms()


def feature(angle):
    turns = jnp.round(angle * (1 / (2 * math.pi)))
    rest = (angle - turns * TWO_PI_HIGH) - turns * TWO_PI_LOW
    q = rest * rest
    p = TERMS[4]
    for term in TERMS[3::-1]:
        p = p * q + term
    return p * p - math.sqrt(2.0)


def move(value, to):
    pairs = []
    for y in range(Y):
        for z in range(Z):
            for c in range(C):
                goal = to(y, z, c)
                if goal is not None:
                    gy, gz, gc = goal
                    pairs.append(((y * Z + z) * C + c, (gy % Y * Z + gz % Z) * C + gc % C))
    return lax.ppermute(value, "tm", pairs)


def swap(value):
    return move(value, lambda y, z, c: (y, z, 1 - c))


def split(value):
    high = value.astype(jnp.bfloat16)
    return high, (value - high.astype(jnp.float32)).astype(jnp.bfloat16)


def contract(left, right):
    return lax.dot_general(left, right, (((0,), (0,)), ((), ())), preferred_element_type=jnp.float32)


def local(snapshots, projection, phase_shift):
    rows, pcs = snapshots.shape
    lags = projection.shape[0] // pcs
    position = lax.axis_index("tm")
    y, z, c = position // (Z * C), position // C % Z, position % C
    x = lax.axis_index("feat")

    width = CWD // Z
    mine = lax.dynamic_slice_in_dim(projection, z * width, width, 1)
    pairs = lambda by: [(i, (i + by) % 4) for i in range(4)]
    parts = [mine] + [lax.ppermute(mine, "feat", pairs(by)) for by in (1, 2, 3)]
    parts = jnp.stack(parts[::-1] + parts[::-1])
    parts = lax.dynamic_slice_in_dim(parts, 3 - x, 4, 0)
    window_projection = jnp.moveaxis(parts, 0, 1).reshape(projection.shape[0], CWD)
    shift_all = lax.all_gather(lax.dynamic_slice_in_dim(phase_shift, z * width, width, 0), "feat", axis=0, tiled=True)

    others = [move(snapshots, lambda y, z, c, by=by: (y, z + by, c)) for by in (1, 2, 3)]
    own = jnp.stack([snapshots] + others)
    other = swap(own)
    pair = jnp.where(c == 0, jnp.stack([own, other], 1), jnp.stack([other, own], 1))
    pair = pair.reshape(4, C * rows, pcs)[::-1]
    slab = lax.dynamic_slice_in_dim(jnp.concatenate([pair, pair]), 3 - z, 4, 0).reshape(-1, pcs)
    count = slab.shape[0]
    before = move(slab[-HALO:], lambda y, z, c: (y + 1, z, c) if y < Y - 1 else None)
    after = move(slab[:HALO], lambda y, z, c: (y - 1, z, c) if y > 0 else None)
    extended = jnp.concatenate([before, slab, after], 0)
    embedded = jnp.concatenate([extended[HALO - k : HALO - k + count + HALO] for k in range(lags)], 1)

    half = projection.shape[1] // C
    own_projection = lax.dynamic_slice_in_dim(projection, c * half, half, 1)
    own_shift = lax.dynamic_slice_in_dim(phase_shift, c * half, half, 0)
    feats = feature(jnp.dot(embedded[:count], own_projection, preferred_element_type=jnp.float32) + own_shift)
    window = feature(jnp.dot(embedded, window_projection, preferred_element_type=jnp.float32) + shift_all)
    later = window[1 : count + 1]
    later = jnp.where((jnp.arange(count) == count - 1)[:, None] & (y == Y - 1), 0.0, later)
    fh, fl = split(feats)

    def product(w):
        wh, wl = split(w)
        return contract(wh, fh) + contract(wl, fh) + contract(wh, fl)

    both = jnp.stack([product(window[:count]), product(later)]).reshape(2, Y, width, half)

    def piece(by):
        return lax.dynamic_index_in_dim(both, (y + by) % Y, 1, keepdims=False)

    far = piece(2)
    up = move(far[0], lambda y, z, c: (y + 1, z, c))
    down = move(far[1], lambda y, z, c: (y - 1, z, c))
    from_below = move(piece(1).at[0].add(up), lambda y, z, c: (y + 1, z, c))
    from_above = move(piece(3).at[1].add(down), lambda y, z, c: (y - 1, z, c))
    total = piece(0) + from_below + from_above

    part = width // C
    theirs = swap(lax.dynamic_slice_in_dim(total, (1 - c) * part, part, 1))
    ours = lax.dynamic_slice_in_dim(total, c * part, part, 1)
    whole = jnp.where(c == 0, jnp.concatenate([ours, theirs], 2), jnp.concatenate([theirs, ours], 2))
    steps = count * Y
    return whole[0].T / steps, whole[1].T / (steps - 1)


def solution(mesh):
    in_specs = (P("tm", None), P(None, "feat"), P("feat"))
    out_specs = (P("feat", "tm"), P("feat", "tm"))
    return jax.shard_map(local, mesh=mesh, in_specs=in_specs, out_specs=out_specs, check_vma=False)
```

```python
import functools
import math

import jax
import jax.numpy as jnp
import numpy as np
from jax import lax
from jax.experimental import pallas as pl
from jax.experimental.pallas import tpu as pltpu
from jax.sharding import PartitionSpec as P

CWD = 512
Y, Z, C = 4, 4, 2
LAGS = 8
BLOCK = 256
CHUNKS = 2

TWO_PI_HIGH = 6.28125
TWO_PI_LOW = 2 * math.pi - TWO_PI_HIGH


def half_cos_terms():
    fit = np.polynomial.chebyshev.Chebyshev.interpolate(
        lambda q: np.cos(np.sqrt(q) / 2), 4, domain=[0.0, (math.pi * 1.0005) ** 2]
    )
    return [float(v * math.sqrt(2 * math.sqrt(2.0))) for v in fit.convert(kind=np.polynomial.Polynomial).coef]


TERMS = half_cos_terms()


def feature(angle):
    turns = jnp.round(angle * (1 / (2 * math.pi)))
    rest = (angle - turns * TWO_PI_HIGH) - turns * TWO_PI_LOW
    q = rest * rest
    p = TERMS[4]
    for term in TERMS[3::-1]:
        p = p * q + term
    return p * p - math.sqrt(2.0)


def split(value):
    high = value.astype(jnp.bfloat16)
    return high, (value - high.astype(jnp.float32)).astype(jnp.bfloat16)


def move(value, to):
    pairs = []
    for y in range(Y):
        for z in range(Z):
            for c in range(C):
                goal = to(y, z, c)
                if goal is not None:
                    gy, gz, gc = goal
                    pairs.append(((y * Z + z) * C + c, (gy % Y * Z + gz % Z) * C + gc % C))
    return lax.ppermute(value, "tm", pairs)


def swap(value):
    return move(value, lambda y, z, c: (y, z, 1 - c))


def around(value, by):
    return lax.ppermute(value, "feat", [(i, (i + by) % 4) for i in range(4)])


def lay_out(x_ref, edge_ref, lagged):
    rows = x_ref.shape[1]
    at = lax.broadcasted_iota(jnp.int32, x_ref.shape[1:], 0)
    for i in range(LAGS):
        lagged[7 + i] = x_ref[i]
    for i in range(1, LAGS):
        older = pltpu.roll(x_ref[i].astype(jnp.float32), 1, 0)
        edge = edge_ref[0, i : i + 1].astype(jnp.float32)
        lagged[i - 1] = jnp.where(at == 0, edge, older).astype(jnp.bfloat16)
    newer = pltpu.roll(x_ref[0].astype(jnp.float32), rows - 1, 0)
    edge = edge_ref[1, 0:1].astype(jnp.float32)
    lagged[15] = jnp.where(at == rows - 1, edge, newer).astype(jnp.bfloat16)


def feats_kernel(place, x_ref, edge_ref, p_ref, shift_ref, high_ref, low_ref, lagged):
    @pl.when(pl.program_id(0) == 0)
    def _():
        lay_out(x_ref, edge_ref, lagged)

    rows = x_ref.shape[1]
    for i in range(LAGS):
        left = jnp.concatenate([lagged[7 + i - k] for k in range(LAGS)], 1)
        angle = jnp.dot(left, p_ref[...], preferred_element_type=jnp.float32) + shift_ref[...]
        high, low = split(feature(angle))
        high_ref[i * rows : (i + 1) * rows, :] = high
        low_ref[i * rows : (i + 1) * rows, :] = low


def feats_of(place, x, edge, projection, shift):
    rows, pcs = x.shape[1:]
    depth, width = projection.shape
    half = width // C
    blocks = half // BLOCK
    out = jax.ShapeDtypeStruct((LAGS * rows, half), jnp.bfloat16)
    return pl.pallas_call(
        feats_kernel,
        out_shape=(out, out),
        grid_spec=pltpu.PrefetchScalarGridSpec(
            num_scalar_prefetch=1,
            grid=(blocks,),
            in_specs=[
                pl.BlockSpec(x.shape, lambda n, s: (0, 0, 0)),
                pl.BlockSpec(edge.shape, lambda n, s: (0, 0, 0)),
                pl.BlockSpec((depth, BLOCK), lambda n, s: (0, s[2] * blocks + n)),
                pl.BlockSpec((1, BLOCK), lambda n, s: (0, s[2] * blocks + n)),
            ],
            out_specs=[pl.BlockSpec((LAGS * rows, BLOCK), lambda n, s: (0, n))] * 2,
            scratch_shapes=[pltpu.VMEM((16, rows, pcs), jnp.bfloat16)],
        ),
        compiler_params=pltpu.CompilerParams(vmem_limit_bytes=40 << 20),
        cost_estimate=pl.CostEstimate(
            flops=2 * LAGS * rows * depth * half, bytes_accessed=2 * depth * half, transcendentals=0
        ),
        name="feats",
    )(place, x, edge, projection, shift)


def window_kernel(place, x_ref, edge_ref, mine_ref, near_ref, swapped_ref, shift_ref, high_ref, low_ref, lagged):
    lay_out(x_ref, edge_ref, lagged)
    rows = x_ref.shape[1]
    y, c = place[0], place[2]
    depth = near_ref.shape[1]
    lags = depth // x_ref.shape[2]
    sides = []
    for own, ref in ((c, near_ref), (1 - c, swapped_ref)):
        mine = mine_ref[pl.ds(pl.multiple_of(own * depth, depth), depth), :]
        sides.append((own * lags, jnp.concatenate([mine, ref[0], ref[1], ref[2]], 1)))
    at = lax.broadcasted_iota(jnp.int32, (rows, 1), 0)
    for i in range(LAGS + 1):
        angle = shift_ref[...]
        for first, right in sides:
            left = jnp.concatenate([lagged[7 + i - k - first] for k in range(lags)], 1)
            angle = angle + jnp.dot(left, right, preferred_element_type=jnp.float32)
        value = feature(angle)
        if i == LAGS:
            value = jnp.where((at == rows - 1) & (y == Y - 1), 0.0, value)
        high, low = split(value.T)
        high_ref[:, i * rows : (i + 1) * rows] = high
        low_ref[:, i * rows : (i + 1) * rows] = low


def window_of(place, x, edge, mine, near, swapped, shift):
    rows, pcs = x.shape[1:]
    out = jax.ShapeDtypeStruct((CWD, (LAGS + 1) * rows), jnp.bfloat16)
    return pl.pallas_call(
        window_kernel,
        out_shape=(out, out),
        in_specs=[pl.BlockSpec(memory_space=pltpu.SMEM)] + [pl.BlockSpec(memory_space=pltpu.VMEM)] * 6,
        out_specs=[pl.BlockSpec(memory_space=pltpu.VMEM)] * 2,
        scratch_shapes=[pltpu.VMEM((16, rows, pcs), jnp.bfloat16)],
        compiler_params=pltpu.CompilerParams(vmem_limit_bytes=40 << 20),
        cost_estimate=pl.CostEstimate(
            flops=2 * (LAGS + 1) * rows * LAGS * pcs * CWD, bytes_accessed=2 * LAGS * pcs * CWD, transcendentals=0
        ),
        name="window",
    )(place, x, edge, mine, near, swapped, shift)


def products_kernel(rows, wh_ref, wl_ref, fh_ref, fl_ref, out_ref):
    count = fh_ref.shape[0]
    for which in range(2):
        span = slice(which * rows, which * rows + count)
        total = jnp.dot(wh_ref[:, span], fh_ref[...], preferred_element_type=jnp.float32)
        total += jnp.dot(wl_ref[:, span], fh_ref[...], preferred_element_type=jnp.float32)
        total += jnp.dot(wh_ref[:, span], fl_ref[...], preferred_element_type=jnp.float32)
        out_ref[which] = total


def products_of(chunk, wh, wl, fh, fl):
    count, half = fh.shape
    width = half // CHUNKS
    steps = width // BLOCK
    return pl.pallas_call(
        functools.partial(products_kernel, wh.shape[1] - count),
        out_shape=jax.ShapeDtypeStruct((2, CWD, width), jnp.float32),
        grid=(steps,),
        in_specs=[pl.BlockSpec(wh.shape, lambda n: (0, 0))] * 2
        + [pl.BlockSpec((count, BLOCK), lambda n: (0, chunk * steps + n))] * 2,
        out_specs=pl.BlockSpec((2, CWD, BLOCK), lambda n: (0, 0, n)),
        compiler_params=pltpu.CompilerParams(vmem_limit_bytes=40 << 20),
        cost_estimate=pl.CostEstimate(flops=12 * count * CWD * width, bytes_accessed=8 << 20, transcendentals=0),
        name="products",
    )(wh, wl, fh, fl)


def local(snapshots, projection, phase_shift):
    rows, pcs = snapshots.shape
    position = lax.axis_index("tm")
    y, z, c = position // (Z * C), position // C % Z, position % C
    x = lax.axis_index("feat")
    place = jnp.stack([y, z, c])

    width = CWD // Z
    depth = projection.shape[0]
    mine = lax.dynamic_slice_in_dim(projection, z * width, width, 1)
    piece = lax.dynamic_slice_in_dim(mine, c * (depth // C), depth // C, 0)
    near = jnp.stack([around(piece, by) for by in (1, 2, 3)])
    swapped = swap(near)
    shift = lax.dynamic_slice_in_dim(phase_shift, z * width, width, 0)[None]
    shifts = jnp.concatenate([shift] + [around(shift, by) for by in (1, 2, 3)], 1)

    phased = jnp.swapaxes(snapshots.reshape(rows // LAGS, LAGS, pcs), 0, 1)
    own = jnp.stack([phased] + [move(phased, lambda y, z, c, by=by: (y, z + by, c)) for by in (1, 2, 3)])
    other = swap(own)
    pair = jnp.where(c == 0, jnp.stack([own, other], 1), jnp.stack([other, own], 1))[::-1]
    slab = lax.dynamic_slice_in_dim(jnp.concatenate([pair, pair]), 3 - z, 4, 0)
    slab = jnp.moveaxis(slab.reshape(Z * C, LAGS, rows // LAGS, pcs), 0, 1).reshape(LAGS, -1, pcs)
    before = move(slab[:, -1], lambda y, z, c: (y + 1, z, c) if y < Y - 1 else None)
    after = move(slab[:, 0], lambda y, z, c: (y - 1, z, c) if y > 0 else None)
    edge = jnp.stack([before, after])

    fh, fl = feats_of(place, slab, edge, projection, phase_shift[None])
    wh, wl = window_of(place, slab, edge, mine, near, swapped, shifts)

    def summed(chunk):
        both = products_of(chunk, wh, wl, fh, fl)

        def toward(by):
            slot = (x - y - by) % 4
            return lax.dynamic_slice_in_dim(both, slot * width, width, 1)

        far = toward(2)
        up = move(far[0], lambda y, z, c: (y + 1, z, c))
        down = move(far[1], lambda y, z, c: (y - 1, z, c))
        from_below = move(toward(1).at[0].add(up), lambda y, z, c: (y + 1, z, c))
        from_above = move(toward(3).at[1].add(down), lambda y, z, c: (y - 1, z, c))
        return toward(0) + from_below + from_above

    total = jnp.concatenate([summed(chunk) for chunk in range(CHUNKS)], 2)

    part = width // C
    theirs = swap(lax.dynamic_slice_in_dim(total, (1 - c) * part, part, 1))
    ours = lax.dynamic_slice_in_dim(total, c * part, part, 1)
    whole = jnp.where(c == 0, jnp.concatenate([ours, theirs], 2), jnp.concatenate([theirs, ours], 2))
    steps = rows * Y * Z * C
    return whole[0].T / steps, whole[1].T / (steps - 1)


def solution(mesh):
    in_specs = (P("tm", None), P(None, "feat"), P("feat"))
    out_specs = (P("feat", "tm"), P("feat", "tm"))
    return jax.shard_map(local, mesh=mesh, in_specs=in_specs, out_specs=out_specs, check_vma=False)
```

```python
import functools
import math

import jax
import jax.numpy as jnp
import numpy as np
from jax import lax
from jax.experimental import pallas as pl
from jax.experimental.pallas import tpu as pltpu
from jax.sharding import PartitionSpec as P

CWD = 512
Y, Z, C = 4, 4, 2
LAGS = 8
BLOCK = 256
VMEM, ALMOST_ALL = 28 << 20, 45 << 20

TWO_PI_HIGH = 6.28125
TWO_PI_LOW = 2 * math.pi - TWO_PI_HIGH


def half_cos_terms():
    fit = np.polynomial.chebyshev.Chebyshev.interpolate(
        lambda q: np.cos(np.sqrt(q) / 2), 4, domain=[0.0, (math.pi * 1.0005) ** 2]
    )
    return [float(v * math.sqrt(2 * math.sqrt(2.0))) for v in fit.convert(kind=np.polynomial.Polynomial).coef]


TERMS = half_cos_terms()


def feature(angle):
    turns = jnp.round(angle * (1 / (2 * math.pi)))
    rest = (angle - turns * TWO_PI_HIGH) - turns * TWO_PI_LOW
    q = rest * rest
    p = TERMS[4]
    for term in TERMS[3::-1]:
        p = p * q + term
    return p * p - math.sqrt(2.0)


def split(value):
    high = value.astype(jnp.bfloat16)
    return high, (value - high.astype(jnp.float32)).astype(jnp.bfloat16)


SCALE, POWER = 32.0, 15.5


def encode(value):
    size = jnp.abs(value) * (1 / SCALE)
    level = jnp.log2(size + jnp.sqrt(size * size + 1.0)) * POWER
    return jnp.exp2(jnp.where(value < 0, -level, level)).astype(jnp.bfloat16)


def decode(code):
    root = jnp.exp2(jnp.log2(code.astype(jnp.float32)) * (1 / POWER))
    return (root - 1.0 / root) * (SCALE / 2)


def move(value, to):
    pairs = []
    for y in range(Y):
        for z in range(Z):
            for c in range(C):
                goal = to(y, z, c)
                if goal is not None:
                    gy, gz, gc = goal
                    pairs.append(((y * Z + z) * C + c, (gy % Y * Z + gz % Z) * C + gc % C))
    return lax.ppermute(value, "tm", pairs)


def swap(value):
    return move(value, lambda y, z, c: (y, z, 1 - c))


def around(value, by):
    return lax.ppermute(value, "feat", [(i, (i + by) % 4) for i in range(4)])


def lag_kernel(place, own_ref, *refs):
    others_ref, edge_ref, lagged = refs[4:]
    z, c = place[1], place[2]
    few = own_ref.shape[1]
    rows = few * Z * C
    mine = [own_ref, *refs[:3]]
    theirs = [refs[3], others_ref.at[0], others_ref.at[1], others_ref.at[2]]
    for core, held in ((c, mine), (1 - c, theirs)):
        for r, ref in enumerate(held):
            start = pl.multiple_of((lax.rem(z - r + Z, Z) * C + core) * few, few)
            lagged[7:15, pl.ds(start, few), :] = ref[...]
    at = lax.broadcasted_iota(jnp.int32, (rows, own_ref.shape[2]), 0)
    for i in range(1, LAGS):
        older = pltpu.roll(lagged[7 + i].astype(jnp.float32), 1, 0)
        edge = edge_ref[0, i : i + 1].astype(jnp.float32)
        lagged[i - 1] = jnp.where(at == 0, edge, older).astype(jnp.bfloat16)
    newer = pltpu.roll(lagged[7].astype(jnp.float32), rows - 1, 0)
    edge = edge_ref[1, 0:1].astype(jnp.float32)
    lagged[15] = jnp.where(at == rows - 1, edge, newer).astype(jnp.bfloat16)


def lag(place, own, other, others, edge):
    few, pcs = other.shape[1:]
    return pl.pallas_call(
        lag_kernel,
        out_shape=jax.ShapeDtypeStruct((16, few * Z * C, pcs), jnp.bfloat16),
        in_specs=[pl.BlockSpec(memory_space=pltpu.SMEM)] + [pl.BlockSpec(memory_space=pltpu.VMEM)] * 7,
        out_specs=pl.BlockSpec(memory_space=pltpu.VMEM),
        compiler_params=pltpu.CompilerParams(vmem_limit_bytes=VMEM),
        cost_estimate=pl.CostEstimate(flops=1 << 20, bytes_accessed=1 << 20, transcendentals=0),
        name="lag",
    )(place, *own, other, others, edge)


def prepare_kernel(place, p_ref, shift_ref, piece_ref, mine_ref, sems):
    z, c = place[1], place[2]
    depth, width = mine_ref.shape
    half = depth // C
    columns = pl.ds(pl.multiple_of(z * width, width), width)
    rows = pl.ds(pl.multiple_of(c * half, half), half)
    whole = pltpu.make_async_copy(p_ref.at[:, columns], mine_ref, sems.at[0])
    part = pltpu.make_async_copy(p_ref.at[rows, columns], piece_ref.at[pl.ds(0, half), :], sems.at[1])
    part.start()
    whole.start()
    rest = shift_ref[:, columns]
    at = lax.broadcasted_iota(jnp.int32, (16, width), 0)
    terms = jnp.zeros((16, width), jnp.float32)
    for i in range(3):
        term = rest.astype(jnp.bfloat16).astype(jnp.float32)
        terms = jnp.where(at == i, term, terms)
        rest = rest - term
    piece_ref[half : half + 16, :] = terms.astype(jnp.bfloat16)
    part.wait()
    whole.wait()


def prepare(place, projection, shift):
    depth, width = projection.shape[0], CWD // Z
    return pl.pallas_call(
        prepare_kernel,
        out_shape=[
            jax.ShapeDtypeStruct((depth // C + 16, width), jnp.bfloat16),
            jax.ShapeDtypeStruct((depth, width), jnp.bfloat16),
        ],
        in_specs=[
            pl.BlockSpec(memory_space=pltpu.SMEM),
            pl.BlockSpec(memory_space=pltpu.HBM),
            pl.BlockSpec(memory_space=pltpu.VMEM),
        ],
        out_specs=[pl.BlockSpec(memory_space=pltpu.VMEM)] * 2,
        scratch_shapes=[pltpu.SemaphoreType.DMA((2,))],
        compiler_params=pltpu.CompilerParams(vmem_limit_bytes=ALMOST_ALL),
        cost_estimate=pl.CostEstimate(flops=0, bytes_accessed=3 << 20, transcendentals=0),
        name="prepare",
    )(place, projection, shift)


def feats_kernel(first, place, lagged, p_ref, shift_ref, high_ref, low_ref, held, sems):
    rows = lagged.shape[1]
    blocks = held.shape[0]
    half = p_ref.shape[1] // C
    copies = []
    for n in range(blocks):
        columns = pl.ds(pl.multiple_of(place[2] * half + (first + n) * BLOCK, BLOCK), BLOCK)
        copies.append((columns, pltpu.make_async_copy(p_ref.at[:, columns], held.at[n], sems.at[n])))
        copies[-1][1].start()
    for n, (columns, copy) in enumerate(copies):
        copy.wait()
        shift = shift_ref[:, columns]
        for i in range(LAGS):
            left = jnp.concatenate([lagged[7 + i - k] for k in range(LAGS)], 1)
            angle = jnp.dot(left, held[n], preferred_element_type=jnp.float32) + shift
            high, low = split(feature(angle))
            to = (slice(i * rows, (i + 1) * rows), slice(n * BLOCK, (n + 1) * BLOCK))
            high_ref[to] = high
            low_ref[to] = low


def feats_of(first, blocks, place, lagged, projection, shift):
    rows = lagged.shape[1]
    depth = projection.shape[0]
    out = jax.ShapeDtypeStruct((LAGS * rows, blocks * BLOCK), jnp.bfloat16)
    return pl.pallas_call(
        functools.partial(feats_kernel, first),
        out_shape=(out, out),
        in_specs=[
            pl.BlockSpec(memory_space=pltpu.SMEM),
            pl.BlockSpec(memory_space=pltpu.VMEM),
            pl.BlockSpec(memory_space=pltpu.HBM),
            pl.BlockSpec(memory_space=pltpu.VMEM),
        ],
        out_specs=[pl.BlockSpec(memory_space=pltpu.VMEM)] * 2,
        scratch_shapes=[pltpu.VMEM((blocks, depth, BLOCK), jnp.bfloat16), pltpu.SemaphoreType.DMA((blocks,))],
        compiler_params=pltpu.CompilerParams(vmem_limit_bytes=ALMOST_ALL),
        cost_estimate=pl.CostEstimate(
            flops=3 * LAGS * rows * depth * blocks * BLOCK, bytes_accessed=2 * depth * blocks * BLOCK, transcendentals=0
        ),
        name="feats",
    )(place, lagged, projection, shift)


def window_kernel(place, *refs):
    lagged, mine_ref = refs[:2]
    near_refs, swapped_refs = refs[2:5], refs[5:8]
    shift_ref, high_ref, low_ref = refs[8:]
    rows = lagged.shape[1]
    y, c, x = place[0], place[2], place[3]
    depth = mine_ref.shape[0] // C
    lags = LAGS // C
    sides = []
    shift = None
    for own, others in ((c, near_refs), (1 - c, swapped_refs)):
        mine = mine_ref[pl.ds(pl.multiple_of(own * depth, depth), depth), :]
        sides.append((own * lags, jnp.concatenate([mine] + [ref[:depth] for ref in others], 1)))
    parts = [jnp.sum(ref[depth : depth + 16].astype(jnp.float32), 0, keepdims=True) for ref in near_refs]
    shift = jnp.concatenate([shift_ref[...]] + parts, 1)
    at = lax.broadcasted_iota(jnp.int32, (rows, 1), 0)
    for i in range(LAGS + 1):
        angle = shift
        for first, right in sides:
            left = jnp.concatenate([lagged[7 + i - k - first] for k in range(lags)], 1)
            angle = angle + jnp.dot(left, right, preferred_element_type=jnp.float32)
        value = feature(angle)
        if i == LAGS:
            value = jnp.where((at == rows - 1) & (y == Y - 1), 0.0, value)
        high, low = split(value.T)
        width = CWD // Y
        for slot, r in enumerate((0, 1, 3, 2)):
            by = lax.rem(x - r - y + 2 * Y, Y)
            to, of = pl.ds(pl.multiple_of(by * width, width), width), slice(slot * width, (slot + 1) * width)
            high_ref[to, i * rows : (i + 1) * rows] = high[of]
            low_ref[to, i * rows : (i + 1) * rows] = low[of]


def window_of(place, lagged, mine, near, swapped, shift):
    rows, pcs = lagged.shape[1:]
    out = jax.ShapeDtypeStruct((CWD, (LAGS + 1) * rows), jnp.bfloat16)
    return pl.pallas_call(
        window_kernel,
        out_shape=(out, out),
        in_specs=[pl.BlockSpec(memory_space=pltpu.SMEM)] + [pl.BlockSpec(memory_space=pltpu.VMEM)] * 9,
        out_specs=[pl.BlockSpec(memory_space=pltpu.VMEM)] * 2,
        compiler_params=pltpu.CompilerParams(vmem_limit_bytes=VMEM),
        cost_estimate=pl.CostEstimate(flops=1 << 33, bytes_accessed=8 << 20, transcendentals=0),
        name="window",
    )(place, lagged, mine, *near, *swapped, shift)


def products_kernel(rows, wh_ref, wl_ref, fh_ref, fl_ref, own_ref, *code_refs):
    count = fh_ref.shape[0]
    width = own_ref.shape[1]
    for which in range(2):
        span = slice(which * rows, which * rows + count)
        total = jnp.dot(wh_ref[:, span], fh_ref[...], preferred_element_type=jnp.float32)
        total += jnp.dot(wl_ref[:, span], fh_ref[...], preferred_element_type=jnp.float32)
        total += jnp.dot(wh_ref[:, span], fl_ref[...], preferred_element_type=jnp.float32)
        own_ref[which] = total[:width]
        for by, ref in enumerate(code_refs, 1):
            ref[which] = encode(total[by * width : (by + 1) * width])


def products_of(wh, wl, fh, fl):
    count, width = fh.shape
    part = CWD // Y
    return pl.pallas_call(
        functools.partial(products_kernel, wh.shape[1] - count),
        out_shape=[jax.ShapeDtypeStruct((2, part, width), jnp.float32)]
        + [jax.ShapeDtypeStruct((2, part, width), jnp.bfloat16)] * 3,
        grid=(width // BLOCK,),
        in_specs=[pl.BlockSpec(memory_space=pltpu.VMEM)] * 2 + [pl.BlockSpec((count, BLOCK), lambda n: (0, n))] * 2,
        out_specs=[pl.BlockSpec((2, part, BLOCK), lambda n: (0, 0, n))] * 4,
        compiler_params=pltpu.CompilerParams(vmem_limit_bytes=VMEM),
        cost_estimate=pl.CostEstimate(flops=12 * count * CWD * width, bytes_accessed=8 << 20, transcendentals=0),
        name="products",
    )(wh, wl, fh, fl)


def after(values, *others):
    return lax.optimization_barrier((values, others))[0]


def local(snapshots, projection, phase_shift):
    rows, pcs = snapshots.shape
    position = lax.axis_index("tm")
    y, z, c = position // (Z * C), position // C % Z, position % C
    x = lax.axis_index("feat")
    place = jnp.stack([y, z, c, x])

    phased = jnp.swapaxes(snapshots.reshape(rows // LAGS, LAGS, pcs), 0, 1)
    ahead, behind, opposite = (move(phased, lambda y, z, c, by=by: (y, z + by, c)) for by in (1, 3, 2))
    own = [phased, ahead, opposite, behind]
    other = swap(phased)
    octets = jnp.stack([jnp.where(c == 1, piece[:, -1], piece[:, 0]) for piece in own])
    octet = lax.dynamic_index_in_dim(octets, jnp.where(c == 1, (z + 1) % Z, z), 0, keepdims=False)

    octet = after(octet, other)
    others = swap(jnp.stack(own[1:]))

    def outward(core):
        def to(y, z, c):
            gy = y + 1 if c == 1 else y - 1
            return (gy, z, c if core == 0 else 1 - c) if 0 <= gy < Y else None

        return move(octet, to)

    straight, crossed = outward(0), outward(1)
    edge = jnp.where(c == 1, jnp.stack([straight, crossed]), jnp.stack([crossed, straight]))

    width = CWD // Z
    phases = phase_shift[None]
    piece, mine = prepare(place, projection, phases)
    shift = lax.dynamic_slice_in_dim(phase_shift, z * width, width, 0)[None]
    piece = after(piece, ahead, behind)
    near = [around(piece, by) for by in (1, 3)]
    lagged = lag(place, own, other, others, edge)
    near.append(around(after(piece, others, edge), 2))

    def feats(first, blocks, *others):
        return feats_of(first, blocks, place, after(lagged, *others), projection, phases)

    def send(codes):
        return [move(codes[by - 1], lambda y, z, c, by=by: (y + by, z, c)) for by in (1, 3, 2)]

    f0 = feats(0, 2)
    near = after(near, f0)
    f1 = feats(2, 1, f0, near)
    swapped = after([swap(v) for v in near], f1)
    w = window_of(place, lagged, mine, near, swapped, shift)
    own0, *codes0 = products_of(*w, *f0)
    sent0 = send(codes0)
    f3 = feats(3, 1, own0)
    own1, *codes1 = products_of(*w, *after(f1, f3, sent0))
    sent1 = send(after(codes1, sent0))
    own2, *codes2 = products_of(*w, *after(f3, sent0, own1))
    sent1 = after(sent1, own2)
    sent2 = send(after(codes2, sent1))
    parts = after([(own0, sent0), (own1, sent1), (own2, sent2)])
    total = jnp.concatenate([own + sum(decode(v) for v in sent) for own, sent in parts], 2)

    part = width // C
    theirs = swap(lax.dynamic_slice_in_dim(total, (1 - c) * part, part, 1))
    ours = lax.dynamic_slice_in_dim(total, c * part, part, 1)
    whole = jnp.where(c == 0, jnp.concatenate([ours, theirs], 2), jnp.concatenate([theirs, ours], 2))
    steps = rows * Y * Z * C
    return whole[0].T / steps, whole[1].T / (steps - 1)


def solution(mesh):
    in_specs = (P("tm", None), P(None, "feat"), P("feat"))
    out_specs = (P("feat", "tm"), P("feat", "tm"))
    return jax.shard_map(local, mesh=mesh, in_specs=in_specs, out_specs=out_specs, check_vma=False)
```

```python
import functools
import math

import jax
import jax.numpy as jnp
import numpy as np
from jax import lax
from jax.experimental import pallas as pl
from jax.experimental.pallas import tpu as pltpu
from jax.sharding import PartitionSpec as P

CWD = 512
Y, Z, C = 4, 4, 2
LAGS = 8
BLOCK = 256
VMEM, ALMOST_ALL = 20 << 20, 42 << 20

ROUNDER = 1.5 * 2**23


def half_cos_terms():
    fit = np.polynomial.chebyshev.Chebyshev.interpolate(
        lambda q: np.cos(np.sqrt(q) * math.pi), 4, domain=[0.0, (0.5 * 1.0005) ** 2]
    )
    return [float(v * math.sqrt(2 * math.sqrt(2.0))) for v in fit.convert(kind=np.polynomial.Polynomial).coef]


TERMS = half_cos_terms()


def feature(projected, shift):
    turns = (projected + shift) * (1 / (2 * math.pi))
    rest = turns - ((turns + ROUNDER) - ROUNDER)
    q = rest * rest
    p = TERMS[4]
    for term in TERMS[3::-1]:
        p = p * q + term
    return p * p - math.sqrt(2.0)


def split(value):
    high = value.astype(jnp.bfloat16)
    return high, (value - high.astype(jnp.float32)).astype(jnp.bfloat16)


SCALE, POWER = 32.0, 15.5


def encode(value):
    size = jnp.abs(value) * (1 / SCALE)
    level = jnp.log2(size + jnp.sqrt(size * size + 1.0)) * POWER
    return jnp.exp2(jnp.where(value < 0, -level, level)).astype(jnp.bfloat16)


def decode(code):
    root = jnp.exp2(jnp.log2(code.astype(jnp.float32)) * (1 / POWER))
    return (root - 1.0 / root) * (SCALE / 2)


def move(value, to):
    pairs = []
    for y in range(Y):
        for z in range(Z):
            for c in range(C):
                goal = to(y, z, c)
                if goal is not None:
                    gy, gz, gc = goal
                    pairs.append(((y * Z + z) * C + c, (gy % Y * Z + gz % Z) * C + gc % C))
    return lax.ppermute(value, "tm", pairs)


def swap(value):
    return move(value, lambda y, z, c: (y, z, 1 - c))


def around(value, by):
    return lax.ppermute(value, "feat", [(i, (i + by) % 4) for i in range(4)])


def lag_kernel(place, own_ref, *refs):
    others_ref, edge_ref, lagged = refs[4:]
    z, c = place[1], place[2]
    few = own_ref.shape[1]
    rows = few * Z * C
    mine = [own_ref, *refs[:3]]
    theirs = [refs[3], others_ref.at[0], others_ref.at[1], others_ref.at[2]]
    for core, held in ((c, mine), (1 - c, theirs)):
        for r, ref in enumerate(held):
            start = pl.multiple_of((lax.rem(z - r + Z, Z) * C + core) * few, few)
            lagged[7:15, pl.ds(start, few), :] = ref[...]
    at = lax.broadcasted_iota(jnp.int32, (rows, own_ref.shape[2]), 0)
    for i in range(1, LAGS):
        older = pltpu.roll(lagged[7 + i].astype(jnp.float32), 1, 0)
        edge = edge_ref[0, i : i + 1].astype(jnp.float32)
        lagged[i - 1] = jnp.where(at == 0, edge, older).astype(jnp.bfloat16)
    newer = pltpu.roll(lagged[7].astype(jnp.float32), rows - 1, 0)
    edge = edge_ref[1, 0:1].astype(jnp.float32)
    lagged[15] = jnp.where(at == rows - 1, edge, newer).astype(jnp.bfloat16)


def lag(place, own, other, others, edge):
    few, pcs = other.shape[1:]
    return pl.pallas_call(
        lag_kernel,
        out_shape=jax.ShapeDtypeStruct((16, few * Z * C, pcs), jnp.bfloat16),
        in_specs=[pl.BlockSpec(memory_space=pltpu.SMEM)] + [pl.BlockSpec(memory_space=pltpu.VMEM)] * 7,
        out_specs=pl.BlockSpec(memory_space=pltpu.VMEM),
        compiler_params=pltpu.CompilerParams(vmem_limit_bytes=VMEM),
        cost_estimate=pl.CostEstimate(flops=1 << 20, bytes_accessed=1 << 20, transcendentals=0),
        name="lag",
    )(place, *own, other, others, edge)


def prepare_kernel(place, p_ref, shift_ref, piece_ref, mine_ref, share_ref, sems):
    z, c = place[1], place[2]
    depth, width = mine_ref.shape
    half = depth // C
    columns = pl.ds(pl.multiple_of(z * width, width), width)
    rows = pl.ds(pl.multiple_of(c * half, half), half)
    whole = pltpu.make_async_copy(p_ref.at[:, columns], mine_ref, sems.at[0])
    part = pltpu.make_async_copy(p_ref.at[rows, columns], piece_ref.at[pl.ds(0, half), :], sems.at[1])
    share = share_ref.shape[1]
    all_rows = pltpu.make_async_copy(
        p_ref.at[:, pl.ds(pl.multiple_of(c * share, share), share)], share_ref, sems.at[2]
    )
    part.start()
    whole.start()
    all_rows.start()
    rest = shift_ref[:, columns]
    at = lax.broadcasted_iota(jnp.int32, (16, width), 0)
    terms = jnp.zeros((16, width), jnp.float32)
    for i in range(3):
        term = rest.astype(jnp.bfloat16).astype(jnp.float32)
        terms = jnp.where(at == i, term, terms)
        rest = rest - term
    piece_ref[half : half + 16, :] = terms.astype(jnp.bfloat16)
    part.wait()
    whole.wait()
    all_rows.wait()


def prepare(place, projection, shift):
    depth, width = projection.shape[0], CWD // Z
    return pl.pallas_call(
        prepare_kernel,
        out_shape=[
            jax.ShapeDtypeStruct((depth // C + 16, width), jnp.bfloat16),
            jax.ShapeDtypeStruct((depth, width), jnp.bfloat16),
            jax.ShapeDtypeStruct((depth, projection.shape[1] // C), jnp.bfloat16),
        ],
        in_specs=[
            pl.BlockSpec(memory_space=pltpu.SMEM),
            pl.BlockSpec(memory_space=pltpu.HBM),
            pl.BlockSpec(memory_space=pltpu.VMEM),
        ],
        out_specs=[pl.BlockSpec(memory_space=pltpu.VMEM)] * 3,
        scratch_shapes=[pltpu.SemaphoreType.DMA((3,))],
        compiler_params=pltpu.CompilerParams(vmem_limit_bytes=ALMOST_ALL),
        cost_estimate=pl.CostEstimate(flops=0, bytes_accessed=3 << 20, transcendentals=0),
        name="prepare",
    )(place, projection, shift)


def feats_kernel(first, place, lagged, p_ref, shift_ref, high_ref, low_ref):
    rows = lagged.shape[1]
    half = p_ref.shape[1]
    for n in range(high_ref.shape[1] // BLOCK):
        column = (first + n) * BLOCK
        right = p_ref[:, column : column + BLOCK]
        shift = shift_ref[:, pl.ds(pl.multiple_of(place[2] * half + column, BLOCK), BLOCK)]
        for i in range(LAGS):
            left = jnp.concatenate([lagged[7 + i - k] for k in range(LAGS)], 1)
            high, low = split(feature(jnp.dot(left, right, preferred_element_type=jnp.float32), shift))
            to = (slice(i * rows, (i + 1) * rows), slice(n * BLOCK, (n + 1) * BLOCK))
            high_ref[to] = high
            low_ref[to] = low


def feats_of(first, blocks, place, lagged, projection, shift):
    rows = lagged.shape[1]
    depth = projection.shape[0]
    out = jax.ShapeDtypeStruct((LAGS * rows, blocks * BLOCK), jnp.bfloat16)
    return pl.pallas_call(
        functools.partial(feats_kernel, first),
        out_shape=(out, out),
        in_specs=[pl.BlockSpec(memory_space=pltpu.SMEM)] + [pl.BlockSpec(memory_space=pltpu.VMEM)] * 3,
        out_specs=[pl.BlockSpec(memory_space=pltpu.VMEM)] * 2,
        compiler_params=pltpu.CompilerParams(vmem_limit_bytes=VMEM),
        cost_estimate=pl.CostEstimate(
            flops=3 * LAGS * rows * depth * blocks * BLOCK, bytes_accessed=2 * depth * blocks * BLOCK, transcendentals=0
        ),
        name="feats",
    )(place, lagged, projection, shift)


def window_kernel(place, *refs):
    lagged, mine_ref = refs[:2]
    near_refs, swapped_refs = refs[2:5], refs[5:8]
    shift_ref, high_ref, low_ref = refs[8:]
    rows = lagged.shape[1]
    y, c, x = place[0], place[2], place[3]
    depth = mine_ref.shape[0] // C
    lags = LAGS // C
    sides = []
    for own, others in ((c, near_refs), (1 - c, swapped_refs)):
        mine = mine_ref[pl.ds(pl.multiple_of(own * depth, depth), depth), :]
        sides.append((own * lags, jnp.concatenate([mine] + [ref[:depth] for ref in others], 1)))
    parts = [jnp.sum(ref[depth : depth + 16].astype(jnp.float32), 0, keepdims=True) for ref in near_refs]
    shift = jnp.concatenate([shift_ref[...]] + parts, 1)
    at = lax.broadcasted_iota(jnp.int32, (rows, 1), 0)
    for i in range(LAGS + 1):
        projected = 0.0
        for first, right in sides:
            left = jnp.concatenate([lagged[7 + i - k - first] for k in range(lags)], 1)
            projected += jnp.dot(left, right, preferred_element_type=jnp.float32)
        value = feature(projected, shift)
        if i == LAGS:
            value = jnp.where((at == rows - 1) & (y == Y - 1), 0.0, value)
        high, low = split(value.T)
        width = CWD // Y
        for slot, r in enumerate((0, 1, 3, 2)):
            by = lax.rem(x - r - y + 2 * Y, Y)
            to, of = pl.ds(pl.multiple_of(by * width, width), width), slice(slot * width, (slot + 1) * width)
            high_ref[to, i * rows : (i + 1) * rows] = high[of]
            low_ref[to, i * rows : (i + 1) * rows] = low[of]


def window_of(place, lagged, mine, near, swapped, shift):
    rows, pcs = lagged.shape[1:]
    out = jax.ShapeDtypeStruct((CWD, (LAGS + 1) * rows), jnp.bfloat16)
    return pl.pallas_call(
        window_kernel,
        out_shape=(out, out),
        in_specs=[pl.BlockSpec(memory_space=pltpu.SMEM)] + [pl.BlockSpec(memory_space=pltpu.VMEM)] * 9,
        out_specs=[pl.BlockSpec(memory_space=pltpu.VMEM)] * 2,
        compiler_params=pltpu.CompilerParams(vmem_limit_bytes=VMEM),
        cost_estimate=pl.CostEstimate(flops=1 << 33, bytes_accessed=8 << 20, transcendentals=0),
        name="window",
    )(place, lagged, mine, *near, *swapped, shift)


def products_kernel(rows, wh_ref, wl_ref, fh_ref, fl_ref, own_ref, *code_refs):
    count = fh_ref.shape[0]
    width = own_ref.shape[1]
    for which in range(2):
        span = slice(which * rows, which * rows + count)
        total = jnp.dot(wh_ref[:, span], fh_ref[...], preferred_element_type=jnp.float32)
        total += jnp.dot(wl_ref[:, span], fh_ref[...], preferred_element_type=jnp.float32)
        total += jnp.dot(wh_ref[:, span], fl_ref[...], preferred_element_type=jnp.float32)
        own_ref[which] = total[:width]
        for by, ref in enumerate(code_refs, 1):
            ref[which] = encode(total[by * width : (by + 1) * width])


def products_of(wh, wl, fh, fl):
    count, width = fh.shape
    part = CWD // Y
    return pl.pallas_call(
        functools.partial(products_kernel, wh.shape[1] - count),
        out_shape=[jax.ShapeDtypeStruct((2, part, width), jnp.float32)]
        + [jax.ShapeDtypeStruct((2, part, width), jnp.bfloat16)] * 3,
        grid=(width // BLOCK,),
        in_specs=[pl.BlockSpec(memory_space=pltpu.VMEM)] * 2 + [pl.BlockSpec((count, BLOCK), lambda n: (0, n))] * 2,
        out_specs=[pl.BlockSpec((2, part, BLOCK), lambda n: (0, 0, n))] * 4,
        compiler_params=pltpu.CompilerParams(vmem_limit_bytes=VMEM),
        cost_estimate=pl.CostEstimate(flops=1 << 20, bytes_accessed=1 << 20, transcendentals=0),
        name="products",
    )(wh, wl, fh, fl)


def after(values, *others):
    return lax.optimization_barrier((values, others))[0]


def local(snapshots, projection, phase_shift):
    rows, pcs = snapshots.shape
    position = lax.axis_index("tm")
    y, z, c = position // (Z * C), position // C % Z, position % C
    x = lax.axis_index("feat")
    place = jnp.stack([y, z, c, x])

    phased = jnp.swapaxes(snapshots.reshape(rows // LAGS, LAGS, pcs), 0, 1)
    ahead, behind, opposite = (move(phased, lambda y, z, c, by=by: (y, z + by, c)) for by in (1, 3, 2))
    own = [phased, ahead, opposite, behind]
    other = swap(phased)
    octets = jnp.stack([jnp.where(c == 1, piece[:, -1], piece[:, 0]) for piece in own])
    octet = lax.dynamic_index_in_dim(octets, jnp.where(c == 1, (z + 1) % Z, z), 0, keepdims=False)

    octet = after(octet, other)
    others = swap(jnp.stack(own[1:]))

    def outward(core):
        def to(y, z, c):
            gy = y + 1 if c == 1 else y - 1
            return (gy, z, c if core == 0 else 1 - c) if 0 <= gy < Y else None

        return move(octet, to)

    straight, crossed = outward(0), outward(1)
    edge = jnp.where(c == 1, jnp.stack([straight, crossed]), jnp.stack([crossed, straight]))

    width = CWD // Z
    phases = phase_shift[None]
    piece, mine, share = prepare(place, projection, phases)
    shift = lax.dynamic_slice_in_dim(phase_shift, z * width, width, 0)[None]
    piece = after(piece, other)
    near = [around(piece, by) for by in (1, 3)]
    lagged = lag(place, own, other, after(others, near), edge)
    near = [*near, around(after(piece, near, others, edge), 2)]

    def feats(first, blocks, *others):
        return feats_of(first, blocks, place, after(lagged, *others), share, phases)

    def send(codes):
        return [move(codes[by - 1], lambda y, z, c, by=by: (y + by, z, c)) for by in (1, 3, 2)]

    f0 = feats(0, 2)
    near = after(near, f0)
    f1 = feats(2, 1, f0, near)
    swapped = after([swap(v) for v in near], f1)
    w = window_of(place, lagged, mine, near, swapped, shift)
    own0, *codes0 = products_of(*w, *f0)
    sent0 = send(codes0)
    f3 = feats(3, 1, own0)
    own1, *codes1 = products_of(*w, *after(f1, f3))
    sent1 = send(after(codes1, sent0))
    own2, *codes2 = products_of(*w, *after(f3, sent0, own1))
    sent1 = after(sent1, own2)
    sent2 = send(after(codes2, sent1))
    parts = after([(own0, sent0), (own1, sent1), (own2, sent2)])
    total = jnp.concatenate([own + sum(decode(v) for v in sent) for own, sent in parts], 2)

    part = width // C
    theirs = swap(lax.dynamic_slice_in_dim(total, (1 - c) * part, part, 1))
    ours = lax.dynamic_slice_in_dim(total, c * part, part, 1)
    whole = jnp.where(c == 0, jnp.concatenate([ours, theirs], 2), jnp.concatenate([theirs, ours], 2))
    steps = rows * Y * Z * C
    return whole[0].T / steps, whole[1].T / (steps - 1)


def solution(mesh):
    in_specs = (P("tm", None), P(None, "feat"), P("feat"))
    out_specs = (P("feat", "tm"), P("feat", "tm"))
    return jax.shard_map(local, mesh=mesh, in_specs=in_specs, out_specs=out_specs, check_vma=False)
```

```python
import functools
import math

import jax
import jax.numpy as jnp
import numpy as np
from jax import lax
from jax.experimental import pallas as pl
from jax.experimental.pallas import tpu as pltpu
from jax.sharding import PartitionSpec as P

CWD = 512
Y, Z, C = 4, 4, 2
LAGS = 8
BLOCK = 256
VMEM, ALMOST_ALL = 20 << 20, 42 << 20

ROUNDER = 1.5 * 2**23


def half_cos_terms():
    fit = np.polynomial.chebyshev.Chebyshev.interpolate(
        lambda q: np.cos(np.sqrt(q) * math.pi), 4, domain=[0.0, (0.5 * 1.0005) ** 2]
    )
    return [float(v * math.sqrt(2 * math.sqrt(2.0))) for v in fit.convert(kind=np.polynomial.Polynomial).coef]


TERMS = half_cos_terms()


def feature(projected, shift):
    turns = (projected + shift) * (1 / (2 * math.pi))
    rest = turns - ((turns + ROUNDER) - ROUNDER)
    q = rest * rest
    p = TERMS[4]
    for term in TERMS[3::-1]:
        p = p * q + term
    return p * p - math.sqrt(2.0)


def split(value):
    high = value.astype(jnp.bfloat16)
    return high, (value - high.astype(jnp.float32)).astype(jnp.bfloat16)


SCALE, POWER = 32.0, 15.5


def encode(value):
    size = jnp.abs(value) * (1 / SCALE)
    level = jnp.log2(size + jnp.sqrt(size * size + 1.0)) * POWER
    return jnp.exp2(jnp.where(value < 0, -level, level)).astype(jnp.bfloat16)


def decode(code):
    root = jnp.exp2(jnp.log2(code.astype(jnp.float32)) * (1 / POWER))
    return (root - 1.0 / root) * (SCALE / 2)


def move(value, to):
    pairs = []
    for y in range(Y):
        for z in range(Z):
            for c in range(C):
                goal = to(y, z, c)
                if goal is not None:
                    gy, gz, gc = goal
                    pairs.append(((y * Z + z) * C + c, (gy % Y * Z + gz % Z) * C + gc % C))
    return lax.ppermute(value, "tm", pairs)


def swap(value):
    return move(value, lambda y, z, c: (y, z, 1 - c))


def around(value, by):
    return lax.ppermute(value, "feat", [(i, (i + by) % 4) for i in range(4)])


def lag_kernel(place, own_ref, *refs):
    others_ref, edge_ref, lagged = refs[4:]
    z, c = place[1], place[2]
    few = own_ref.shape[1]
    rows = few * Z * C
    mine = [own_ref, *refs[:3]]
    theirs = [refs[3], others_ref.at[0], others_ref.at[1], others_ref.at[2]]
    for core, held in ((c, mine), (1 - c, theirs)):
        for r, ref in enumerate(held):
            start = pl.multiple_of((lax.rem(z - r + Z, Z) * C + core) * few, few)
            lagged[7:15, pl.ds(start, few), :] = ref[...]
    at = lax.broadcasted_iota(jnp.int32, (rows, own_ref.shape[2]), 0)
    for i in range(1, LAGS):
        older = pltpu.roll(lagged[7 + i].astype(jnp.float32), 1, 0)
        edge = edge_ref[0, i : i + 1].astype(jnp.float32)
        lagged[i - 1] = jnp.where(at == 0, edge, older).astype(jnp.bfloat16)
    newer = pltpu.roll(lagged[7].astype(jnp.float32), rows - 1, 0)
    edge = edge_ref[1, 0:1].astype(jnp.float32)
    lagged[15] = jnp.where(at == rows - 1, edge, newer).astype(jnp.bfloat16)


def lag(place, own, other, others, edge):
    few, pcs = other.shape[1:]
    return pl.pallas_call(
        lag_kernel,
        out_shape=jax.ShapeDtypeStruct((16, few * Z * C, pcs), jnp.bfloat16),
        in_specs=[pl.BlockSpec(memory_space=pltpu.SMEM)] + [pl.BlockSpec(memory_space=pltpu.VMEM)] * 7,
        out_specs=pl.BlockSpec(memory_space=pltpu.VMEM),
        compiler_params=pltpu.CompilerParams(vmem_limit_bytes=VMEM),
        cost_estimate=pl.CostEstimate(flops=1 << 20, bytes_accessed=1 << 20, transcendentals=0),
        name="lag",
    )(place, *own, other, others, edge)


def prepare_kernel(place, p_ref, shift_ref, piece_ref, mine_ref, sems):
    z, c = place[1], place[2]
    depth, width = mine_ref.shape
    half = depth // C
    columns = pl.ds(pl.multiple_of(z * width, width), width)
    rows = pl.ds(pl.multiple_of(c * half, half), half)
    whole = pltpu.make_async_copy(p_ref.at[:, columns], mine_ref, sems.at[0])
    part = pltpu.make_async_copy(p_ref.at[rows, columns], piece_ref.at[pl.ds(0, half), :], sems.at[1])
    part.start()
    whole.start()
    rest = shift_ref[:, columns]
    at = lax.broadcasted_iota(jnp.int32, (16, width), 0)
    terms = jnp.zeros((16, width), jnp.float32)
    for i in range(3):
        term = rest.astype(jnp.bfloat16).astype(jnp.float32)
        terms = jnp.where(at == i, term, terms)
        rest = rest - term
    piece_ref[half : half + 16, :] = terms.astype(jnp.bfloat16)
    part.wait()
    whole.wait()


def prepare(place, projection, shift):
    depth, width = projection.shape[0], CWD // Z
    return pl.pallas_call(
        prepare_kernel,
        out_shape=[
            jax.ShapeDtypeStruct((depth // C + 16, width), jnp.bfloat16),
            jax.ShapeDtypeStruct((depth, width), jnp.bfloat16),
        ],
        in_specs=[
            pl.BlockSpec(memory_space=pltpu.SMEM),
            pl.BlockSpec(memory_space=pltpu.HBM),
            pl.BlockSpec(memory_space=pltpu.VMEM),
        ],
        out_specs=[pl.BlockSpec(memory_space=pltpu.VMEM)] * 2,
        scratch_shapes=[pltpu.SemaphoreType.DMA((2,))],
        compiler_params=pltpu.CompilerParams(vmem_limit_bytes=ALMOST_ALL),
        cost_estimate=pl.CostEstimate(flops=0, bytes_accessed=3 << 20, transcendentals=0),
        name="prepare",
    )(place, projection, shift)


def share_kernel(place, p_ref, share_ref, sem):
    width = share_ref.shape[1]
    copy = pltpu.make_async_copy(p_ref.at[:, pl.ds(pl.multiple_of(place[2] * width, width), width)], share_ref, sem)
    copy.start()
    copy.wait()


def share_of(place, projection):
    depth, width = projection.shape
    return pl.pallas_call(
        share_kernel,
        out_shape=jax.ShapeDtypeStruct((depth, width // C), jnp.bfloat16),
        in_specs=[pl.BlockSpec(memory_space=pltpu.SMEM), pl.BlockSpec(memory_space=pltpu.HBM)],
        out_specs=pl.BlockSpec(memory_space=pltpu.VMEM),
        scratch_shapes=[pltpu.SemaphoreType.DMA],
        compiler_params=pltpu.CompilerParams(vmem_limit_bytes=ALMOST_ALL),
        cost_estimate=pl.CostEstimate(flops=0, bytes_accessed=8 << 20, transcendentals=0),
        name="share",
    )(place, projection)


def feats_kernel(first, place, lagged, p_ref, shift_ref, high_ref, low_ref):
    rows = lagged.shape[1]
    half = p_ref.shape[1]
    pairs = LAGS // 2
    for n in range(high_ref.shape[1] // BLOCK):
        column = (first + n) * BLOCK
        right = p_ref[:, column : column + BLOCK]
        shift = shift_ref[:, pl.ds(pl.multiple_of(place[2] * half + column, BLOCK), BLOCK)]

        def put(at, value):
            to = (slice(at * rows, (at + 1) * rows), slice(n * BLOCK, (n + 1) * BLOCK))
            high_ref[to], low_ref[to] = split(value)

        for i in range(LAGS):
            left = jnp.concatenate([lagged[7 + i - k] for k in range(LAGS)], 1)
            value = feature(jnp.dot(left, right, preferred_element_type=jnp.float32), shift)
            put(i // 2 + (i % 2) * 2 * pairs, value)
            if i % 2 == 0:
                even = value
            else:
                put(i // 2 + pairs, even + value)


def feats_of(first, blocks, place, lagged, projection, shift):
    rows = lagged.shape[1]
    depth = projection.shape[0]
    out = jax.ShapeDtypeStruct((LAGS * 3 // 2 * rows, blocks * BLOCK), jnp.bfloat16)
    return pl.pallas_call(
        functools.partial(feats_kernel, first),
        out_shape=(out, out),
        in_specs=[pl.BlockSpec(memory_space=pltpu.SMEM)] + [pl.BlockSpec(memory_space=pltpu.VMEM)] * 3,
        out_specs=[pl.BlockSpec(memory_space=pltpu.VMEM)] * 2,
        compiler_params=pltpu.CompilerParams(vmem_limit_bytes=VMEM),
        cost_estimate=pl.CostEstimate(
            flops=3 * LAGS * rows * depth * blocks * BLOCK, bytes_accessed=2 * depth * blocks * BLOCK, transcendentals=0
        ),
        name="feats",
    )(place, lagged, projection, shift)


def window_kernel(place, *refs):
    lagged, mine_ref = refs[:2]
    near_refs, swapped_refs = refs[2:5], refs[5:8]
    shift_ref, high_ref, low_ref = refs[8:]
    rows = lagged.shape[1]
    y, c, x = place[0], place[2], place[3]
    depth = mine_ref.shape[0] // C
    lags = LAGS // C
    sides = []
    for own, others in ((c, near_refs), (1 - c, swapped_refs)):
        mine = mine_ref[pl.ds(pl.multiple_of(own * depth, depth), depth), :]
        sides.append((own * lags, jnp.concatenate([mine] + [ref[:depth] for ref in others], 1)))
    parts = [jnp.sum(ref[depth : depth + 16].astype(jnp.float32), 0, keepdims=True) for ref in near_refs]
    shift = jnp.concatenate([shift_ref[...]] + parts, 1)
    at = lax.broadcasted_iota(jnp.int32, (rows, 1), 0)

    def put(place_at, value):
        high, low = split(value)
        width = CWD // Y
        columns = slice(place_at * rows, (place_at + 1) * rows)
        for slot, r in enumerate((0, 1, 3, 2)):
            by = lax.rem(x - r - y + 2 * Y, Y)
            to, of = pl.ds(pl.multiple_of(by * width, width), width), slice(slot * width, (slot + 1) * width)
            high_ref[to, columns] = high[of]
            low_ref[to, columns] = low[of]

    for i in range(LAGS + 1):
        if i < LAGS:
            projected = 0.0
            for first, right in sides:
                left = jnp.concatenate([lagged[7 + i - k - first] for k in range(lags)], 1)
                if i == LAGS - 1:
                    last = [lagged[8 + i - k - first, rows - 16 : rows, :] for k in range(lags)]
                    left = jnp.concatenate([left, jnp.concatenate(last, 1)], 0)
                projected += jnp.dot(left, right, preferred_element_type=jnp.float32)
            values = feature(projected, shift)
            value = values[:rows]
            if i == 0:
                start = value
        else:
            last = jnp.where(y == Y - 1, 0.0, values[rows + 15 : rows + 16])
            value = jnp.where(at == rows - 1, last, pltpu.roll(start, rows - 1, 0))
        value = value.T
        if i > 0:
            put((i - 1) // 2 + ((i - 1) % 2) * LAGS, previous - value)
        if i % 2 == 1:
            put(i // 2 + LAGS // 2, value)
        previous = value


def window_of(place, lagged, mine, near, swapped, shift):
    rows, pcs = lagged.shape[1:]
    out = jax.ShapeDtypeStruct((CWD, LAGS * 3 // 2 * rows), jnp.bfloat16)
    return pl.pallas_call(
        window_kernel,
        out_shape=(out, out),
        in_specs=[pl.BlockSpec(memory_space=pltpu.SMEM)] + [pl.BlockSpec(memory_space=pltpu.VMEM)] * 9,
        out_specs=[pl.BlockSpec(memory_space=pltpu.VMEM)] * 2,
        compiler_params=pltpu.CompilerParams(vmem_limit_bytes=VMEM),
        cost_estimate=pl.CostEstimate(flops=1 << 33, bytes_accessed=8 << 20, transcendentals=0),
        name="window",
    )(place, lagged, mine, *near, *swapped, shift)


def products_kernel(wh_ref, wl_ref, fh_ref, fl_ref, own_ref, *code_refs):
    third = fh_ref.shape[0] // 3
    width = own_ref.shape[1]
    for n in range(fh_ref.shape[1] // BLOCK):
        columns = slice(n * BLOCK, (n + 1) * BLOCK)
        terms = []
        for part in range(3):
            span = slice(part * third, (part + 1) * third)
            total = jnp.dot(wh_ref[:, span], fh_ref[span, columns], preferred_element_type=jnp.float32)
            total += jnp.dot(wl_ref[:, span], fh_ref[span, columns], preferred_element_type=jnp.float32)
            total += jnp.dot(wh_ref[:, span], fl_ref[span, columns], preferred_element_type=jnp.float32)
            terms.append(total)
        for which, total in enumerate((terms[0] + terms[1], terms[1] - terms[2])):
            own_ref[which, :, columns] = total[:width]
            for by, ref in enumerate(code_refs, 1):
                ref[which, :, columns] = encode(total[by * width : (by + 1) * width])


def products_of(wh, wl, fh, fl):
    width = fh.shape[1]
    part = CWD // Y
    return pl.pallas_call(
        products_kernel,
        out_shape=[jax.ShapeDtypeStruct((2, part, width), jnp.float32)]
        + [jax.ShapeDtypeStruct((2, part, width), jnp.bfloat16)] * 3,
        in_specs=[pl.BlockSpec(memory_space=pltpu.VMEM)] * 4,
        out_specs=[pl.BlockSpec(memory_space=pltpu.VMEM)] * 4,
        compiler_params=pltpu.CompilerParams(vmem_limit_bytes=VMEM),
        cost_estimate=pl.CostEstimate(flops=1 << 20, bytes_accessed=1 << 20, transcendentals=0),
        name="products",
    )(wh, wl, fh, fl)


def after(values, *others):
    return lax.optimization_barrier((values, others))[0]


def local(snapshots, projection, phase_shift):
    rows, pcs = snapshots.shape
    position = lax.axis_index("tm")
    y, z, c = position // (Z * C), position // C % Z, position % C
    x = lax.axis_index("feat")
    place = jnp.stack([y, z, c, x])

    phased = jnp.swapaxes(snapshots.reshape(rows // LAGS, LAGS, pcs), 0, 1)
    ahead, behind, opposite = (move(phased, lambda y, z, c, by=by: (y, z + by, c)) for by in (1, 3, 2))
    own = [phased, ahead, opposite, behind]
    other = swap(phased)
    octets = jnp.stack([jnp.where(c == 1, piece[:, -1], piece[:, 0]) for piece in own])
    octet = lax.dynamic_index_in_dim(octets, jnp.where(c == 1, (z + 1) % Z, z), 0, keepdims=False)

    octet = after(octet, other)
    others = swap(jnp.stack(own[1:]))

    def outward(core):
        def to(y, z, c):
            gy = y + 1 if c == 1 else y - 1
            return (gy, z, c if core == 0 else 1 - c) if 0 <= gy < Y else None

        return move(octet, to)

    straight, crossed = outward(0), outward(1)
    edge = jnp.where(c == 1, jnp.stack([straight, crossed]), jnp.stack([crossed, straight]))

    width = CWD // Z
    phases = phase_shift[None]
    piece, mine = prepare(place, projection, phases)
    share = share_of(after(place, ahead), projection)
    shift = lax.dynamic_slice_in_dim(phase_shift, z * width, width, 0)[None]
    piece = after(piece, other)
    near = [around(piece, by) for by in (1, 3)]
    lagged = lag(place, own, other, after(others, near), edge)
    swapped = [swap(v) for v in after(near, lagged)]
    near = [*near, around(after(piece, lagged), 2)]

    def feats(first, blocks, *others):
        return feats_of(first, blocks, place, after(lagged, *others), share, phases)

    def send(codes):
        return [move(codes[by - 1], lambda y, z, c, by=by: (y + by, z, c)) for by in (1, 3, 2)]

    f0 = feats(0, 2, shift)
    swapped = [*after(swapped, f0), swap(after(near[2], f0))]
    w = window_of(place, lagged, mine, near, swapped, shift)
    own0, *codes0 = products_of(*w, *f0)
    sent0 = send(codes0)
    f1 = feats(2, 2, own0)
    own1, *codes1 = products_of(*w, *after(f1, own0))
    sent0 = after(sent0, own1)
    sent1 = send(after(codes1, sent0))
    part = width // C

    def finish(chunks):
        total = jnp.concatenate([own + sum(decode(v) for v in sent) for own, sent in chunks], 2)
        low, high = total[:, :part], total[:, part:]
        return jnp.where(c == 1, high, low), swap(jnp.where(c == 1, low, high))

    most = finish(after([(own0, sent0)], own1))
    rest = finish([(own1, sent1)])
    ours, theirs = (jnp.concatenate(v, 2) for v in zip(most, rest))
    whole = jnp.where(c == 1, jnp.concatenate([theirs, ours], 2), jnp.concatenate([ours, theirs], 2))
    steps = rows * Y * Z * C
    return whole[0].T / steps, whole[1].T / (steps - 1)


def solution(mesh):
    in_specs = (P("tm", None), P(None, "feat"), P("feat"))
    out_specs = (P("feat", "tm"), P("feat", "tm"))
    return jax.shard_map(local, mesh=mesh, in_specs=in_specs, out_specs=out_specs, check_vma=False)
```

```python
import functools
import math

import jax
import jax.numpy as jnp
import numpy as np
from jax import lax
from jax.experimental import pallas as pl
from jax.experimental.pallas import tpu as pltpu
from jax.sharding import PartitionSpec as P

CWD = 512
Y, Z, C = 4, 4, 2
LAGS = 8
BLOCK = 256
VMEM, ALMOST_ALL = 20 << 20, 42 << 20

ROUNDER = 1.5 * 2**23


def half_cos_terms():
    fit = np.polynomial.chebyshev.Chebyshev.interpolate(
        lambda q: np.cos(np.sqrt(q) * math.pi), 4, domain=[0.0, (0.5 * 1.0005) ** 2]
    )
    return [float(v * math.sqrt(2 * math.sqrt(2.0))) for v in fit.convert(kind=np.polynomial.Polynomial).coef]


TERMS = half_cos_terms()


def feature(projected, shift):
    turns = (projected + shift) * (1 / (2 * math.pi))
    rest = turns - ((turns + ROUNDER) - ROUNDER)
    q = rest * rest
    p = TERMS[4]
    for term in TERMS[3::-1]:
        p = p * q + term
    return p * p - math.sqrt(2.0)


def split(value):
    high = value.astype(jnp.bfloat16)
    return high, (value - high.astype(jnp.float32)).astype(jnp.bfloat16)


SCALE, POWER = 32.0, 15.5


def encode(value):
    size = jnp.abs(value) * (1 / SCALE)
    level = jnp.log2(size + jnp.sqrt(size * size + 1.0)) * POWER
    return jnp.exp2(jnp.where(value < 0, -level, level)).astype(jnp.bfloat16)


def decode(code):
    root = jnp.exp2(jnp.log2(code.astype(jnp.float32)) * (1 / POWER))
    return (root - 1.0 / root) * (SCALE / 2)


def move(value, to):
    pairs = []
    for y in range(Y):
        for z in range(Z):
            for c in range(C):
                goal = to(y, z, c)
                if goal is not None:
                    gy, gz, gc = goal
                    pairs.append(((y * Z + z) * C + c, (gy % Y * Z + gz % Z) * C + gc % C))
    return lax.ppermute(value, "tm", pairs)


def swap(value):
    return move(value, lambda y, z, c: (y, z, 1 - c))


def around(value, by):
    return lax.ppermute(value, "feat", [(i, (i + by) % 4) for i in range(4)])


def lag_kernel(place, own_ref, *refs):
    others_ref, edge_ref, lagged = refs[4:]
    z, c = place[1], place[2]
    few = own_ref.shape[1]
    rows = few * Z * C
    mine = [own_ref, *refs[:3]]
    theirs = [refs[3], others_ref.at[0], others_ref.at[1], others_ref.at[2]]
    for core, held in ((c, mine), (1 - c, theirs)):
        for r, ref in enumerate(held):
            start = pl.multiple_of((lax.rem(z - r + Z, Z) * C + core) * few, few)
            lagged[7:15, pl.ds(start, few), :] = ref[...]
    at = lax.broadcasted_iota(jnp.int32, (rows, own_ref.shape[2]), 0)
    for i in range(1, LAGS):
        older = pltpu.roll(lagged[7 + i].astype(jnp.float32), 1, 0)
        edge = edge_ref[0, i : i + 1].astype(jnp.float32)
        lagged[i - 1] = jnp.where(at == 0, edge, older).astype(jnp.bfloat16)
    newer = pltpu.roll(lagged[7].astype(jnp.float32), rows - 1, 0)
    edge = edge_ref[1, 0:1].astype(jnp.float32)
    lagged[15] = jnp.where(at == rows - 1, edge, newer).astype(jnp.bfloat16)


def lag(place, own, other, others, edge):
    few, pcs = other.shape[1:]
    return pl.pallas_call(
        lag_kernel,
        out_shape=jax.ShapeDtypeStruct((16, few * Z * C, pcs), jnp.bfloat16),
        in_specs=[pl.BlockSpec(memory_space=pltpu.SMEM)] + [pl.BlockSpec(memory_space=pltpu.VMEM)] * 7,
        out_specs=pl.BlockSpec(memory_space=pltpu.VMEM),
        compiler_params=pltpu.CompilerParams(vmem_limit_bytes=VMEM),
        cost_estimate=pl.CostEstimate(flops=1 << 20, bytes_accessed=1 << 20, transcendentals=0),
        name="lag",
    )(place, *own, other, others, edge)


def prepare_kernel(place, p_ref, shift_ref, piece_ref, mine_ref, sems):
    z, c = place[1], place[2]
    depth, width = mine_ref.shape
    half = depth // C
    columns = pl.ds(pl.multiple_of(z * width, width), width)
    rows = pl.ds(pl.multiple_of(c * half, half), half)
    whole = pltpu.make_async_copy(p_ref.at[:, columns], mine_ref, sems.at[0])
    part = pltpu.make_async_copy(p_ref.at[rows, columns], piece_ref.at[pl.ds(0, half), :], sems.at[1])
    part.start()
    whole.start()
    rest = shift_ref[:, columns]
    at = lax.broadcasted_iota(jnp.int32, (16, width), 0)
    terms = jnp.zeros((16, width), jnp.float32)
    for i in range(3):
        term = rest.astype(jnp.bfloat16).astype(jnp.float32)
        terms = jnp.where(at == i, term, terms)
        rest = rest - term
    piece_ref[half : half + 16, :] = terms.astype(jnp.bfloat16)
    part.wait()
    whole.wait()


def prepare(place, projection, shift):
    depth, width = projection.shape[0], CWD // Z
    return pl.pallas_call(
        prepare_kernel,
        out_shape=[
            jax.ShapeDtypeStruct((depth // C + 16, width), jnp.bfloat16),
            jax.ShapeDtypeStruct((depth, width), jnp.bfloat16),
        ],
        in_specs=[
            pl.BlockSpec(memory_space=pltpu.SMEM),
            pl.BlockSpec(memory_space=pltpu.HBM),
            pl.BlockSpec(memory_space=pltpu.VMEM),
        ],
        out_specs=[pl.BlockSpec(memory_space=pltpu.VMEM)] * 2,
        scratch_shapes=[pltpu.SemaphoreType.DMA((2,))],
        compiler_params=pltpu.CompilerParams(vmem_limit_bytes=ALMOST_ALL),
        cost_estimate=pl.CostEstimate(flops=0, bytes_accessed=3 << 20, transcendentals=0),
        name="prepare",
    )(place, projection, shift)


def share_kernel(part, place, p_ref, share_ref, sem):
    width = share_ref.shape[1]
    start = pl.multiple_of((place[2] * 2 + part) * width, width)
    copy = pltpu.make_async_copy(p_ref.at[:, pl.ds(start, width)], share_ref, sem)
    copy.start()
    copy.wait()


def share_of(part, place, projection):
    depth, width = projection.shape
    return pl.pallas_call(
        functools.partial(share_kernel, part),
        out_shape=jax.ShapeDtypeStruct((depth, width // C // 2), jnp.bfloat16),
        in_specs=[pl.BlockSpec(memory_space=pltpu.SMEM), pl.BlockSpec(memory_space=pltpu.HBM)],
        out_specs=pl.BlockSpec(memory_space=pltpu.VMEM),
        scratch_shapes=[pltpu.SemaphoreType.DMA],
        compiler_params=pltpu.CompilerParams(vmem_limit_bytes=ALMOST_ALL),
        cost_estimate=pl.CostEstimate(flops=0, bytes_accessed=8 << 20, transcendentals=0),
        name="share",
    )(place, projection)


def feats_kernel(first, place, lagged, p_ref, shift_ref, high_ref, low_ref):
    rows = lagged.shape[1]
    half = shift_ref.shape[1] // C
    pairs = LAGS // 2
    for n in range(high_ref.shape[1] // BLOCK):
        column = (first + n) * BLOCK
        right = p_ref[:, n * BLOCK : (n + 1) * BLOCK]
        shift = shift_ref[:, pl.ds(pl.multiple_of(place[2] * half + column, BLOCK), BLOCK)]

        def put(at, value):
            to = (slice(at * rows, (at + 1) * rows), slice(n * BLOCK, (n + 1) * BLOCK))
            high_ref[to], low_ref[to] = split(value)

        for i in range(LAGS):
            left = jnp.concatenate([lagged[7 + i - k] for k in range(LAGS)], 1)
            value = feature(jnp.dot(left, right, preferred_element_type=jnp.float32), shift)
            put(i // 2 + (i % 2) * 2 * pairs, value)
            if i % 2 == 0:
                even = value
            else:
                put(i // 2 + pairs, even + value)


def feats_of(first, blocks, place, lagged, projection, shift):
    rows = lagged.shape[1]
    depth = projection.shape[0]
    out = jax.ShapeDtypeStruct((LAGS * 3 // 2 * rows, blocks * BLOCK), jnp.bfloat16)
    return pl.pallas_call(
        functools.partial(feats_kernel, first),
        out_shape=(out, out),
        in_specs=[pl.BlockSpec(memory_space=pltpu.SMEM)] + [pl.BlockSpec(memory_space=pltpu.VMEM)] * 3,
        out_specs=[pl.BlockSpec(memory_space=pltpu.VMEM)] * 2,
        compiler_params=pltpu.CompilerParams(vmem_limit_bytes=VMEM),
        cost_estimate=pl.CostEstimate(
            flops=3 * LAGS * rows * depth * blocks * BLOCK, bytes_accessed=2 * depth * blocks * BLOCK, transcendentals=0
        ),
        name="feats",
    )(place, lagged, projection, shift)


def window_kernel(place, *refs):
    lagged, mine_ref = refs[:2]
    near_refs, swapped_refs = refs[2:5], refs[5:8]
    shift_ref, high_ref, low_ref = refs[8:]
    rows = lagged.shape[1]
    y, c, x = place[0], place[2], place[3]
    depth = mine_ref.shape[0] // C
    lags = LAGS // C
    sides = []
    for own, others in ((c, near_refs), (1 - c, swapped_refs)):
        mine = mine_ref[pl.ds(pl.multiple_of(own * depth, depth), depth), :]
        sides.append((own * lags, jnp.concatenate([mine] + [ref[:depth] for ref in others], 1)))
    parts = [jnp.sum(ref[depth : depth + 16].astype(jnp.float32), 0, keepdims=True) for ref in near_refs]
    shift = jnp.concatenate([shift_ref[...]] + parts, 1)
    at = lax.broadcasted_iota(jnp.int32, (rows, 1), 0)

    def put(place_at, value):
        high, low = split(value)
        width = CWD // Y
        columns = slice(place_at * rows, (place_at + 1) * rows)
        for slot, r in enumerate((0, 1, 3, 2)):
            by = lax.rem(x - r - y + 2 * Y, Y)
            to, of = pl.ds(pl.multiple_of(by * width, width), width), slice(slot * width, (slot + 1) * width)
            high_ref[to, columns] = high[of]
            low_ref[to, columns] = low[of]

    for i in range(LAGS + 1):
        if i < LAGS:
            projected = 0.0
            for first, right in sides:
                left = jnp.concatenate([lagged[7 + i - k - first] for k in range(lags)], 1)
                if i == LAGS - 1:
                    last = [lagged[8 + i - k - first, rows - 16 : rows, :] for k in range(lags)]
                    left = jnp.concatenate([left, jnp.concatenate(last, 1)], 0)
                projected += jnp.dot(left, right, preferred_element_type=jnp.float32)
            values = feature(projected, shift)
            value = values[:rows]
            if i == 0:
                start = value
        else:
            last = jnp.where(y == Y - 1, 0.0, values[rows + 15 : rows + 16])
            value = jnp.where(at == rows - 1, last, pltpu.roll(start, rows - 1, 0))
        value = value.T
        if i > 0:
            put((i - 1) // 2 + ((i - 1) % 2) * LAGS, previous - value)
        if i % 2 == 1:
            put(i // 2 + LAGS // 2, value)
        previous = value


def window_of(place, lagged, mine, near, swapped, shift):
    rows, pcs = lagged.shape[1:]
    out = jax.ShapeDtypeStruct((CWD, LAGS * 3 // 2 * rows), jnp.bfloat16)
    return pl.pallas_call(
        window_kernel,
        out_shape=(out, out),
        in_specs=[pl.BlockSpec(memory_space=pltpu.SMEM)] + [pl.BlockSpec(memory_space=pltpu.VMEM)] * 9,
        out_specs=[pl.BlockSpec(memory_space=pltpu.VMEM)] * 2,
        compiler_params=pltpu.CompilerParams(vmem_limit_bytes=VMEM),
        cost_estimate=pl.CostEstimate(flops=1 << 33, bytes_accessed=8 << 20, transcendentals=0),
        name="window",
    )(place, lagged, mine, *near, *swapped, shift)


def products_kernel(wh_ref, wl_ref, fh_ref, fl_ref, own_ref, *code_refs):
    third = fh_ref.shape[0] // 3
    width = own_ref.shape[1]
    for n in range(fh_ref.shape[1] // BLOCK):
        columns = slice(n * BLOCK, (n + 1) * BLOCK)
        terms = []
        for part in range(3):
            span = slice(part * third, (part + 1) * third)
            total = jnp.dot(wh_ref[:, span], fh_ref[span, columns], preferred_element_type=jnp.float32)
            total += jnp.dot(wl_ref[:, span], fh_ref[span, columns], preferred_element_type=jnp.float32)
            total += jnp.dot(wh_ref[:, span], fl_ref[span, columns], preferred_element_type=jnp.float32)
            terms.append(total)
        for which, total in enumerate((terms[0] + terms[1], terms[1] - terms[2])):
            own_ref[which, :, columns] = total[:width]
            for by, ref in enumerate(code_refs, 1):
                ref[which, :, columns] = encode(total[by * width : (by + 1) * width])


def products_of(wh, wl, fh, fl):
    width = fh.shape[1]
    part = CWD // Y
    return pl.pallas_call(
        products_kernel,
        out_shape=[jax.ShapeDtypeStruct((2, part, width), jnp.float32)]
        + [jax.ShapeDtypeStruct((2, part, width), jnp.bfloat16)] * 3,
        in_specs=[pl.BlockSpec(memory_space=pltpu.VMEM)] * 4,
        out_specs=[pl.BlockSpec(memory_space=pltpu.VMEM)] * 4,
        compiler_params=pltpu.CompilerParams(vmem_limit_bytes=VMEM),
        cost_estimate=pl.CostEstimate(flops=1 << 20, bytes_accessed=1 << 20, transcendentals=0),
        name="products",
    )(wh, wl, fh, fl)


def after(values, *others):
    return lax.optimization_barrier((values, others))[0]


def local(snapshots, projection, phase_shift):
    rows, pcs = snapshots.shape
    position = lax.axis_index("tm")
    y, z, c = position // (Z * C), position // C % Z, position % C
    x = lax.axis_index("feat")
    place = jnp.stack([y, z, c, x])

    phased = jnp.swapaxes(snapshots.reshape(rows // LAGS, LAGS, pcs), 0, 1)
    ahead, behind, opposite = (move(phased, lambda y, z, c, by=by: (y, z + by, c)) for by in (1, 3, 2))
    own = [phased, ahead, opposite, behind]
    other = swap(phased)
    octets = jnp.stack([jnp.where(c == 1, piece[:, -1], piece[:, 0]) for piece in own])
    octet = lax.dynamic_index_in_dim(octets, jnp.where(c == 1, (z + 1) % Z, z), 0, keepdims=False)

    octet = after(octet, other)
    others = swap(jnp.stack(own[1:]))

    def outward(core):
        def to(y, z, c):
            gy = y + 1 if c == 1 else y - 1
            return (gy, z, c if core == 0 else 1 - c) if 0 <= gy < Y else None

        return move(octet, to)

    straight, crossed = outward(0), outward(1)
    edge = jnp.where(c == 1, jnp.stack([straight, crossed]), jnp.stack([crossed, straight]))

    width = CWD // Z
    phases = phase_shift[None]
    piece, mine = prepare(place, projection, phases)
    share = share_of(0, after(place, ahead), projection)
    shift = lax.dynamic_slice_in_dim(phase_shift, z * width, width, 0)[None]
    piece = after(piece, other)
    near = [around(piece, by) for by in (1, 3)]
    lagged = lag(place, own, other, after(others, near), edge)
    swapped = [swap(v) for v in after(near, lagged)]
    near = [*near, around(after(piece, lagged), 2)]

    def feats(first, blocks, share, *others):
        return feats_of(first, blocks, place, after(lagged, *others), share, phases)

    def send(codes):
        return [move(codes[by - 1], lambda y, z, c, by=by: (y + by, z, c)) for by in (1, 3, 2)]

    f0 = feats(0, 2, share, shift)
    share = share_of(1, after(place, f0), projection)
    swapped = [*after(swapped, f0), swap(after(near[2], f0))]
    w = window_of(place, lagged, mine, near, after(swapped, share), shift)
    own0, *codes0 = products_of(*w, *f0)
    sent0 = send(codes0)
    f1 = feats(2, 2, share, own0)
    own1, *codes1 = products_of(*w, *after(f1, own0))
    sent0 = after(sent0, own1)
    sent1 = send(after(codes1, sent0))
    part = width // C

    def finish(chunks):
        total = jnp.concatenate([own + sum(decode(v) for v in sent) for own, sent in chunks], 2)
        low, high = total[:, :part], total[:, part:]
        return jnp.where(c == 1, high, low), swap(jnp.where(c == 1, low, high))

    most = finish(after([(own0, sent0)], own1))
    rest = finish([(own1, sent1)])
    ours, theirs = (jnp.concatenate(v, 2) for v in zip(most, rest))
    whole = jnp.where(c == 1, jnp.concatenate([theirs, ours], 2), jnp.concatenate([ours, theirs], 2))
    steps = rows * Y * Z * C
    return whole[0].T / steps, whole[1].T / (steps - 1)


def solution(mesh):
    in_specs = (P("tm", None), P(None, "feat"), P("feat"))
    out_specs = (P("feat", "tm"), P("feat", "tm"))
    return jax.shard_map(local, mesh=mesh, in_specs=in_specs, out_specs=out_specs, check_vma=False)
```

```python
import functools
import math

import jax
import jax.numpy as jnp
import numpy as np
from jax import lax
from jax.experimental import pallas as pl
from jax.experimental.pallas import tpu as pltpu
from jax.sharding import PartitionSpec as P

CWD = 512
Y, Z, C = 4, 4, 2
LAGS = 8
BLOCK = 256
VMEM, ALMOST_ALL = 20 << 20, 42 << 20

ROUNDER = 1.5 * 2**23


def half_cos_terms():
    fit = np.polynomial.chebyshev.Chebyshev.interpolate(
        lambda q: np.cos(np.sqrt(q) * math.pi), 4, domain=[0.0, (0.5 * 1.0005) ** 2]
    )
    return [float(v * math.sqrt(2 * math.sqrt(2.0))) for v in fit.convert(kind=np.polynomial.Polynomial).coef]


TERMS = half_cos_terms()


def feature(projected, shift):
    turns = (projected + shift) * (1 / (2 * math.pi))
    rest = turns - ((turns + ROUNDER) - ROUNDER)
    q = rest * rest
    p = TERMS[4]
    for term in TERMS[3::-1]:
        p = p * q + term
    return p * p - math.sqrt(2.0)


def split(value):
    high = value.astype(jnp.bfloat16)
    return high, (value - high.astype(jnp.float32)).astype(jnp.bfloat16)


SCALE, POWER = 32.0, 15.5


def encode(value):
    size = jnp.abs(value) * (1 / SCALE)
    level = jnp.log2(size + jnp.sqrt(size * size + 1.0)) * POWER
    return jnp.exp2(jnp.where(value < 0, -level, level)).astype(jnp.bfloat16)


def decode(code):
    root = jnp.exp2(jnp.log2(code.astype(jnp.float32)) * (1 / POWER))
    return (root - 1.0 / root) * (SCALE / 2)


def move(value, to):
    pairs = []
    for y in range(Y):
        for z in range(Z):
            for c in range(C):
                goal = to(y, z, c)
                if goal is not None:
                    gy, gz, gc = goal
                    pairs.append(((y * Z + z) * C + c, (gy % Y * Z + gz % Z) * C + gc % C))
    return lax.ppermute(value, "tm", pairs)


def swap(value):
    return move(value, lambda y, z, c: (y, z, 1 - c))


def around(value, by):
    return lax.ppermute(value, "feat", [(i, (i + by) % 4) for i in range(4)])


def lag_kernel(place, own_ref, *refs):
    others_ref, edge_ref, lagged = refs[4:]
    z, c = place[1], place[2]
    few = own_ref.shape[1]
    rows = few * Z * C
    mine = [own_ref, *refs[:3]]
    theirs = [refs[3], others_ref.at[0], others_ref.at[1], others_ref.at[2]]
    for core, held in ((c, mine), (1 - c, theirs)):
        for r, ref in enumerate(held):
            start = pl.multiple_of((lax.rem(z - r + Z, Z) * C + core) * few, few)
            lagged[7:15, pl.ds(start, few), :] = ref[...]
    at = lax.broadcasted_iota(jnp.int32, (rows, own_ref.shape[2]), 0)
    for i in range(1, LAGS):
        older = pltpu.roll(lagged[7 + i].astype(jnp.float32), 1, 0)
        edge = edge_ref[0, i : i + 1].astype(jnp.float32)
        lagged[i - 1] = jnp.where(at == 0, edge, older).astype(jnp.bfloat16)
    newer = pltpu.roll(lagged[7].astype(jnp.float32), rows - 1, 0)
    edge = edge_ref[1, 0:1].astype(jnp.float32)
    lagged[15] = jnp.where(at == rows - 1, edge, newer).astype(jnp.bfloat16)


def lag(place, own, other, others, edge):
    few, pcs = other.shape[1:]
    return pl.pallas_call(
        lag_kernel,
        out_shape=jax.ShapeDtypeStruct((16, few * Z * C, pcs), jnp.bfloat16),
        in_specs=[pl.BlockSpec(memory_space=pltpu.SMEM)] + [pl.BlockSpec(memory_space=pltpu.VMEM)] * 7,
        out_specs=pl.BlockSpec(memory_space=pltpu.VMEM),
        compiler_params=pltpu.CompilerParams(vmem_limit_bytes=VMEM),
        cost_estimate=pl.CostEstimate(flops=1 << 20, bytes_accessed=1 << 20, transcendentals=0),
        name="lag",
    )(place, *own, other, others, edge)


def prepare_kernel(place, p_ref, shift_ref, piece_ref, mine_ref, sems):
    z, c = place[1], place[2]
    depth, width = mine_ref.shape
    half = depth // C
    columns = pl.ds(pl.multiple_of(z * width, width), width)
    rows = pl.ds(pl.multiple_of(c * half, half), half)
    whole = pltpu.make_async_copy(p_ref.at[:, columns], mine_ref, sems.at[0])
    part = pltpu.make_async_copy(p_ref.at[rows, columns], piece_ref.at[pl.ds(0, half), :], sems.at[1])
    part.start()
    whole.start()
    rest = shift_ref[:, columns]
    at = lax.broadcasted_iota(jnp.int32, (16, width), 0)
    terms = jnp.zeros((16, width), jnp.float32)
    for i in range(3):
        term = rest.astype(jnp.bfloat16).astype(jnp.float32)
        terms = jnp.where(at == i, term, terms)
        rest = rest - term
    piece_ref[half : half + 16, :] = terms.astype(jnp.bfloat16)
    part.wait()
    whole.wait()


def prepare(place, projection, shift):
    depth, width = projection.shape[0], CWD // Z
    return pl.pallas_call(
        prepare_kernel,
        out_shape=[
            jax.ShapeDtypeStruct((depth // C + 16, width), jnp.bfloat16),
            jax.ShapeDtypeStruct((depth, width), jnp.bfloat16),
        ],
        in_specs=[
            pl.BlockSpec(memory_space=pltpu.SMEM),
            pl.BlockSpec(memory_space=pltpu.HBM),
            pl.BlockSpec(memory_space=pltpu.VMEM),
        ],
        out_specs=[pl.BlockSpec(memory_space=pltpu.VMEM)] * 2,
        scratch_shapes=[pltpu.SemaphoreType.DMA((2,))],
        compiler_params=pltpu.CompilerParams(vmem_limit_bytes=ALMOST_ALL),
        cost_estimate=pl.CostEstimate(flops=0, bytes_accessed=3 << 20, transcendentals=0),
        name="prepare",
    )(place, projection, shift)


def share_kernel(part, place, p_ref, share_ref, sem):
    width = share_ref.shape[1]
    start = pl.multiple_of((place[2] * 2 + part) * width, width)
    copy = pltpu.make_async_copy(p_ref.at[:, pl.ds(start, width)], share_ref, sem)
    copy.start()
    copy.wait()


def share_of(part, place, projection):
    depth, width = projection.shape
    return pl.pallas_call(
        functools.partial(share_kernel, part),
        out_shape=jax.ShapeDtypeStruct((depth, width // C // 2), jnp.bfloat16),
        in_specs=[pl.BlockSpec(memory_space=pltpu.SMEM), pl.BlockSpec(memory_space=pltpu.HBM)],
        out_specs=pl.BlockSpec(memory_space=pltpu.VMEM),
        scratch_shapes=[pltpu.SemaphoreType.DMA],
        compiler_params=pltpu.CompilerParams(vmem_limit_bytes=ALMOST_ALL),
        cost_estimate=pl.CostEstimate(flops=0, bytes_accessed=8 << 20, transcendentals=0),
        name="share",
    )(place, projection)


def feats_kernel(first, place, lagged, p_ref, shift_ref, high_ref, low_ref):
    rows = lagged.shape[1]
    half = shift_ref.shape[1] // C
    pairs = LAGS // 2
    for n in range(high_ref.shape[1] // BLOCK):
        column = (first + n) * BLOCK
        right = p_ref[:, n * BLOCK : (n + 1) * BLOCK]
        shift = shift_ref[:, pl.ds(pl.multiple_of(place[2] * half + column, BLOCK), BLOCK)]

        def put(at, value):
            to = (slice(at * rows, (at + 1) * rows), slice(n * BLOCK, (n + 1) * BLOCK))
            high_ref[to], low_ref[to] = split(value)

        for i in range(LAGS):
            left = jnp.concatenate([lagged[7 + i - k] for k in range(LAGS)], 1)
            value = feature(jnp.dot(left, right, preferred_element_type=jnp.float32), shift)
            put(i // 2 + (i % 2) * 2 * pairs, value)
            if i % 2 == 0:
                even = value
            else:
                put(i // 2 + pairs, even + value)


def feats_of(first, blocks, place, lagged, projection, shift):
    rows = lagged.shape[1]
    depth = projection.shape[0]
    out = jax.ShapeDtypeStruct((LAGS * 3 // 2 * rows, blocks * BLOCK), jnp.bfloat16)
    return pl.pallas_call(
        functools.partial(feats_kernel, first),
        out_shape=(out, out),
        in_specs=[pl.BlockSpec(memory_space=pltpu.SMEM)] + [pl.BlockSpec(memory_space=pltpu.VMEM)] * 3,
        out_specs=[pl.BlockSpec(memory_space=pltpu.VMEM)] * 2,
        compiler_params=pltpu.CompilerParams(vmem_limit_bytes=VMEM),
        cost_estimate=pl.CostEstimate(
            flops=3 * LAGS * rows * depth * blocks * BLOCK, bytes_accessed=2 * depth * blocks * BLOCK, transcendentals=0
        ),
        name="feats",
    )(place, lagged, projection, shift)


def window_kernel(place, *refs):
    lagged, mine_ref = refs[:2]
    near_refs, swapped_refs = refs[2:5], refs[5:8]
    shift_ref, high_ref, low_ref = refs[8:]
    rows = lagged.shape[1]
    y, c, x = place[0], place[2], place[3]
    depth = mine_ref.shape[0] // C
    lags = LAGS // C
    sides = []
    for own, others in ((c, near_refs), (1 - c, swapped_refs)):
        mine = mine_ref[pl.ds(pl.multiple_of(own * depth, depth), depth), :]
        sides.append((own * lags, jnp.concatenate([mine] + [ref[:depth] for ref in others], 1)))
    parts = [jnp.sum(ref[depth : depth + 16].astype(jnp.float32), 0, keepdims=True) for ref in near_refs]
    shift = jnp.concatenate([shift_ref[...]] + parts, 1)
    at = lax.broadcasted_iota(jnp.int32, (rows, 1), 0)

    def put(place_at, value):
        high, low = split(value)
        width = CWD // Y
        columns = slice(place_at * rows, (place_at + 1) * rows)
        for slot, r in enumerate((0, 1, 3, 2)):
            by = lax.rem(x - r - y + 2 * Y, Y)
            to, of = pl.ds(pl.multiple_of(by * width, width), width), slice(slot * width, (slot + 1) * width)
            high_ref[to, columns] = high[of]
            low_ref[to, columns] = low[of]

    for i in range(LAGS + 1):
        if i < LAGS:
            projected = 0.0
            for first, right in sides:
                left = jnp.concatenate([lagged[7 + i - k - first] for k in range(lags)], 1)
                if i == LAGS - 1:
                    last = [lagged[8 + i - k - first, rows - 16 : rows, :] for k in range(lags)]
                    left = jnp.concatenate([left, jnp.concatenate(last, 1)], 0)
                projected += jnp.dot(left, right, preferred_element_type=jnp.float32)
            values = feature(projected, shift)
            value = values[:rows]
            if i == 0:
                start = value
        else:
            last = jnp.where(y == Y - 1, 0.0, values[rows + 15 : rows + 16])
            value = jnp.where(at == rows - 1, last, pltpu.roll(start, rows - 1, 0))
        value = value.T
        if i > 0:
            put((i - 1) // 2 + ((i - 1) % 2) * LAGS, previous - value)
        if i % 2 == 1:
            put(i // 2 + LAGS // 2, value)
        previous = value


def window_of(place, lagged, mine, near, swapped, shift):
    rows, pcs = lagged.shape[1:]
    out = jax.ShapeDtypeStruct((CWD, LAGS * 3 // 2 * rows), jnp.bfloat16)
    return pl.pallas_call(
        window_kernel,
        out_shape=(out, out),
        in_specs=[pl.BlockSpec(memory_space=pltpu.SMEM)] + [pl.BlockSpec(memory_space=pltpu.VMEM)] * 9,
        out_specs=[pl.BlockSpec(memory_space=pltpu.VMEM)] * 2,
        compiler_params=pltpu.CompilerParams(vmem_limit_bytes=VMEM),
        cost_estimate=pl.CostEstimate(flops=1 << 33, bytes_accessed=8 << 20, transcendentals=0),
        name="window",
    )(place, lagged, mine, *near, *swapped, shift)


def products_kernel(wh_ref, wl_ref, fh_ref, fl_ref, own_ref, *code_refs):
    third = fh_ref.shape[0] // 3
    width = own_ref.shape[1]
    for n in range(fh_ref.shape[1] // BLOCK):
        columns = slice(n * BLOCK, (n + 1) * BLOCK)
        terms = []
        for part in range(3):
            span = slice(part * third, (part + 1) * third)
            total = jnp.dot(wh_ref[:, span], fh_ref[span, columns], preferred_element_type=jnp.float32)
            total += jnp.dot(wl_ref[:, span], fh_ref[span, columns], preferred_element_type=jnp.float32)
            total += jnp.dot(wh_ref[:, span], fl_ref[span, columns], preferred_element_type=jnp.float32)
            terms.append(total)
        for which, total in enumerate((terms[0] + terms[1], terms[1] - terms[2])):
            own_ref[which, :, columns] = total[:width]
            for by, ref in enumerate(code_refs, 1):
                ref[which, :, columns] = encode(total[by * width : (by + 1) * width])


def products_of(wh, wl, fh, fl):
    width = fh.shape[1]
    part = CWD // Y
    return pl.pallas_call(
        products_kernel,
        out_shape=[jax.ShapeDtypeStruct((2, part, width), jnp.float32)]
        + [jax.ShapeDtypeStruct((2, part, width), jnp.bfloat16)] * 3,
        in_specs=[pl.BlockSpec(memory_space=pltpu.VMEM)] * 4,
        out_specs=[pl.BlockSpec(memory_space=pltpu.VMEM)] * 4,
        compiler_params=pltpu.CompilerParams(vmem_limit_bytes=VMEM),
        cost_estimate=pl.CostEstimate(flops=1 << 20, bytes_accessed=1 << 20, transcendentals=0),
        name="products",
    )(wh, wl, fh, fl)


def after(values, *others):
    return lax.optimization_barrier((values, others))[0]


def local(snapshots, projection, phase_shift):
    rows, pcs = snapshots.shape
    position = lax.axis_index("tm")
    y, z, c = position // (Z * C), position // C % Z, position % C
    x = lax.axis_index("feat")
    place = jnp.stack([y, z, c, x])

    phased = jnp.swapaxes(snapshots.reshape(rows // LAGS, LAGS, pcs), 0, 1)
    ahead, behind, opposite = (move(phased, lambda y, z, c, by=by: (y, z + by, c)) for by in (1, 3, 2))
    own = [phased, ahead, opposite, behind]
    other = swap(phased)
    octets = jnp.stack([jnp.where(c == 1, piece[:, -1], piece[:, 0]) for piece in own])
    octet = lax.dynamic_index_in_dim(octets, jnp.where(c == 1, (z + 1) % Z, z), 0, keepdims=False)

    octet = after(octet, other)
    others = swap(jnp.stack(own[1:]))

    def outward(core):
        def to(y, z, c):
            gy = y + 1 if c == 1 else y - 1
            return (gy, z, c if core == 0 else 1 - c) if 0 <= gy < Y else None

        return move(octet, to)

    straight, crossed = outward(0), outward(1)
    edge = jnp.where(c == 1, jnp.stack([straight, crossed]), jnp.stack([crossed, straight]))

    width = CWD // Z
    phases = phase_shift[None]
    piece, mine = prepare(place, projection, phases)
    share = share_of(0, after(place, ahead), projection)
    shift = lax.dynamic_slice_in_dim(phase_shift, z * width, width, 0)[None]
    piece = after(piece, other)
    near = [around(piece, by) for by in (1, 3)]
    lagged = lag(place, own, other, after(others, near), edge)
    near = [*near, around(after(piece, lagged), 2)]

    def feats(first, blocks, share, *others):
        return feats_of(first, blocks, place, after(lagged, *others), share, phases)

    def send(codes):
        return [move(codes[by - 1], lambda y, z, c, by=by: (y + by, z, c)) for by in (1, 3, 2)]

    f0 = feats(0, 2, share, shift)
    share = share_of(1, after(place, f0), projection)
    swapped = [swap(v) for v in after(near, f0)]
    w = window_of(place, lagged, mine, near, after(swapped, share), shift)
    own0, *codes0 = products_of(*w, *f0)
    sent0 = send(codes0)
    f1 = feats(2, 2, share, own0)
    own1, *codes1 = products_of(*w, *after(f1, own0))
    sent0 = after(sent0, own1)
    sent1 = send(after(codes1, sent0))
    part = width // C

    def finish(chunks):
        total = jnp.concatenate([own + sum(decode(v) for v in sent) for own, sent in chunks], 2)
        low, high = total[:, :part], total[:, part:]
        return jnp.where(c == 1, high, low), swap(jnp.where(c == 1, low, high))

    most = finish(after([(own0, sent0)], own1))
    rest = finish([(own1, sent1)])
    ours, theirs = (jnp.concatenate(v, 2) for v in zip(most, rest))
    whole = jnp.where(c == 1, jnp.concatenate([theirs, ours], 2), jnp.concatenate([ours, theirs], 2))
    steps = rows * Y * Z * C
    return whole[0].T / steps, whole[1].T / (steps - 1)


def solution(mesh):
    in_specs = (P("tm", None), P(None, "feat"), P("feat"))
    out_specs = (P("feat", "tm"), P("feat", "tm"))
    return jax.shard_map(local, mesh=mesh, in_specs=in_specs, out_specs=out_specs, check_vma=False)
```

```python
import functools
import math

import jax
import jax.numpy as jnp
import numpy as np
from jax import lax
from jax.experimental import pallas as pl
from jax.experimental.pallas import tpu as pltpu
from jax.sharding import PartitionSpec as P

CWD = 512
Y, Z, C = 4, 4, 2
LAGS = 8
BLOCK = 256
VMEM, ALMOST_ALL = 20 << 20, 42 << 20

ROUNDER = 1.5 * 2**23


def half_cos_terms():
    fit = np.polynomial.chebyshev.Chebyshev.interpolate(
        lambda q: np.cos(np.sqrt(q) * math.pi), 4, domain=[0.0, (0.5 * 1.0005) ** 2]
    )
    return [float(v * math.sqrt(2 * math.sqrt(2.0))) for v in fit.convert(kind=np.polynomial.Polynomial).coef]


TERMS = half_cos_terms()


def feature(projected, shift):
    turns = (projected + shift) * (1 / (2 * math.pi))
    rest = turns - ((turns + ROUNDER) - ROUNDER)
    q = rest * rest
    p = TERMS[4]
    for term in TERMS[3::-1]:
        p = p * q + term
    return p * p - math.sqrt(2.0)


def split(value):
    high = value.astype(jnp.bfloat16)
    return high, (value - high.astype(jnp.float32)).astype(jnp.bfloat16)


SCALE, POWER = 32.0, 15.5


def encode(value):
    size = jnp.abs(value) * (1 / SCALE)
    level = jnp.log2(size + jnp.sqrt(size * size + 1.0)) * POWER
    return jnp.exp2(jnp.where(value < 0, -level, level)).astype(jnp.bfloat16)


def decode(code):
    root = jnp.exp2(jnp.log2(code.astype(jnp.float32)) * (1 / POWER))
    return (root - 1.0 / root) * (SCALE / 2)


def move(value, to):
    pairs = []
    for y in range(Y):
        for z in range(Z):
            for c in range(C):
                goal = to(y, z, c)
                if goal is not None:
                    gy, gz, gc = goal
                    pairs.append(((y * Z + z) * C + c, (gy % Y * Z + gz % Z) * C + gc % C))
    return lax.ppermute(value, "tm", pairs)


def swap(value):
    return move(value, lambda y, z, c: (y, z, 1 - c))


def around(value, by):
    return lax.ppermute(value, "feat", [(i, (i + by) % 4) for i in range(4)])


def lag_kernel(place, own_ref, *refs):
    others_ref, edge_ref, lagged = refs[4:]
    z, c = place[1], place[2]
    few = own_ref.shape[1]
    rows = few * Z * C
    mine = [own_ref, *refs[:3]]
    theirs = [refs[3], others_ref.at[0], others_ref.at[1], others_ref.at[2]]
    for core, held in ((c, mine), (1 - c, theirs)):
        for r, ref in enumerate(held):
            start = pl.multiple_of((lax.rem(z - r + Z, Z) * C + core) * few, few)
            lagged[7:15, pl.ds(start, few), :] = ref[...]
    at = lax.broadcasted_iota(jnp.int32, (rows, own_ref.shape[2]), 0)
    for i in range(1, LAGS):
        older = pltpu.roll(lagged[7 + i].astype(jnp.float32), 1, 0)
        edge = edge_ref[0, i : i + 1].astype(jnp.float32)
        lagged[i - 1] = jnp.where(at == 0, edge, older).astype(jnp.bfloat16)
    newer = pltpu.roll(lagged[7].astype(jnp.float32), rows - 1, 0)
    edge = edge_ref[1, 0:1].astype(jnp.float32)
    lagged[15] = jnp.where(at == rows - 1, edge, newer).astype(jnp.bfloat16)


def lag(place, own, other, others, edge):
    few, pcs = other.shape[1:]
    return pl.pallas_call(
        lag_kernel,
        out_shape=jax.ShapeDtypeStruct((16, few * Z * C, pcs), jnp.bfloat16),
        in_specs=[pl.BlockSpec(memory_space=pltpu.SMEM)] + [pl.BlockSpec(memory_space=pltpu.VMEM)] * 7,
        out_specs=pl.BlockSpec(memory_space=pltpu.VMEM),
        compiler_params=pltpu.CompilerParams(vmem_limit_bytes=VMEM),
        cost_estimate=pl.CostEstimate(flops=1 << 20, bytes_accessed=1 << 20, transcendentals=0),
        name="lag",
    )(place, *own, other, others, edge)


def prepare_kernel(place, p_ref, shift_ref, piece_ref, mine_ref, sems):
    z, c = place[1], place[2]
    depth, width = mine_ref.shape
    half = depth // C
    columns = pl.ds(pl.multiple_of(z * width, width), width)
    rows = pl.ds(pl.multiple_of(c * half, half), half)
    whole = pltpu.make_async_copy(p_ref.at[:, columns], mine_ref, sems.at[0])
    part = pltpu.make_async_copy(p_ref.at[rows, columns], piece_ref.at[pl.ds(0, half), :], sems.at[1])
    part.start()
    whole.start()
    rest = shift_ref[:, columns]
    at = lax.broadcasted_iota(jnp.int32, (16, width), 0)
    terms = jnp.zeros((16, width), jnp.float32)
    for i in range(3):
        term = rest.astype(jnp.bfloat16).astype(jnp.float32)
        terms = jnp.where(at == i, term, terms)
        rest = rest - term
    piece_ref[half : half + 16, :] = terms.astype(jnp.bfloat16)
    part.wait()
    whole.wait()


def prepare(place, projection, shift):
    depth, width = projection.shape[0], CWD // Z
    return pl.pallas_call(
        prepare_kernel,
        out_shape=[
            jax.ShapeDtypeStruct((depth // C + 16, width), jnp.bfloat16),
            jax.ShapeDtypeStruct((depth, width), jnp.bfloat16),
        ],
        in_specs=[
            pl.BlockSpec(memory_space=pltpu.SMEM),
            pl.BlockSpec(memory_space=pltpu.HBM),
            pl.BlockSpec(memory_space=pltpu.VMEM),
        ],
        out_specs=[pl.BlockSpec(memory_space=pltpu.VMEM)] * 2,
        scratch_shapes=[pltpu.SemaphoreType.DMA((2,))],
        compiler_params=pltpu.CompilerParams(vmem_limit_bytes=ALMOST_ALL),
        cost_estimate=pl.CostEstimate(flops=0, bytes_accessed=3 << 20, transcendentals=0),
        name="prepare",
    )(place, projection, shift)


def share_kernel(part, place, p_ref, share_ref, sem):
    width = share_ref.shape[1]
    start = pl.multiple_of((place[2] * 2 + part) * width, width)
    copy = pltpu.make_async_copy(p_ref.at[:, pl.ds(start, width)], share_ref, sem)
    copy.start()
    copy.wait()


def share_of(part, place, projection):
    depth, width = projection.shape
    return pl.pallas_call(
        functools.partial(share_kernel, part),
        out_shape=jax.ShapeDtypeStruct((depth, width // C // 2), jnp.bfloat16),
        in_specs=[pl.BlockSpec(memory_space=pltpu.SMEM), pl.BlockSpec(memory_space=pltpu.HBM)],
        out_specs=pl.BlockSpec(memory_space=pltpu.VMEM),
        scratch_shapes=[pltpu.SemaphoreType.DMA],
        compiler_params=pltpu.CompilerParams(vmem_limit_bytes=ALMOST_ALL),
        cost_estimate=pl.CostEstimate(flops=0, bytes_accessed=8 << 20, transcendentals=0),
        name="share",
    )(place, projection)


def feats_kernel(first, place, lagged, p_ref, shift_ref, high_ref, low_ref):
    rows = lagged.shape[1]
    half = shift_ref.shape[1] // C
    pairs = LAGS // 2
    for n in range(high_ref.shape[1] // BLOCK):
        column = (first + n) * BLOCK
        right = p_ref[:, n * BLOCK : (n + 1) * BLOCK]
        shift = shift_ref[:, pl.ds(pl.multiple_of(place[2] * half + column, BLOCK), BLOCK)]

        def put(at, value):
            to = (slice(at * rows, (at + 1) * rows), slice(n * BLOCK, (n + 1) * BLOCK))
            high_ref[to], low_ref[to] = split(value)

        for i in range(LAGS):
            left = jnp.concatenate([lagged[7 + i - k] for k in range(LAGS)], 1)
            value = feature(jnp.dot(left, right, preferred_element_type=jnp.float32), shift)
            put(i // 2 + (i % 2) * 2 * pairs, value)
            if i % 2 == 0:
                even = value
            else:
                put(i // 2 + pairs, even + value)


def feats_of(first, blocks, place, lagged, projection, shift):
    rows = lagged.shape[1]
    depth = projection.shape[0]
    out = jax.ShapeDtypeStruct((LAGS * 3 // 2 * rows, blocks * BLOCK), jnp.bfloat16)
    return pl.pallas_call(
        functools.partial(feats_kernel, first),
        out_shape=(out, out),
        in_specs=[pl.BlockSpec(memory_space=pltpu.SMEM)] + [pl.BlockSpec(memory_space=pltpu.VMEM)] * 3,
        out_specs=[pl.BlockSpec(memory_space=pltpu.VMEM)] * 2,
        compiler_params=pltpu.CompilerParams(vmem_limit_bytes=VMEM),
        cost_estimate=pl.CostEstimate(
            flops=3 * LAGS * rows * depth * blocks * BLOCK, bytes_accessed=2 * depth * blocks * BLOCK, transcendentals=0
        ),
        name="feats",
    )(place, lagged, projection, shift)


def window_kernel(place, *refs):
    lagged, mine_ref = refs[:2]
    near_refs, swapped_refs = refs[2:5], refs[5:8]
    shift_ref, high_ref, low_ref = refs[8:]
    rows = lagged.shape[1]
    y, c, x = place[0], place[2], place[3]
    depth = mine_ref.shape[0] // C
    lags = LAGS // C
    sides = []
    for own, others in ((c, near_refs), (1 - c, swapped_refs)):
        mine = mine_ref[pl.ds(pl.multiple_of(own * depth, depth), depth), :]
        sides.append((own * lags, jnp.concatenate([mine] + [ref[:depth] for ref in others], 1)))
    parts = [jnp.sum(ref[depth : depth + 16].astype(jnp.float32), 0, keepdims=True) for ref in near_refs]
    shift = jnp.concatenate([shift_ref[...]] + parts, 1)
    at = lax.broadcasted_iota(jnp.int32, (rows, 1), 0)

    def put(place_at, value):
        high, low = split(value)
        width = CWD // Y
        columns = slice(place_at * rows, (place_at + 1) * rows)
        for slot, r in enumerate((0, 1, 3, 2)):
            by = lax.rem(x - r - y + 2 * Y, Y)
            to, of = pl.ds(pl.multiple_of(by * width, width), width), slice(slot * width, (slot + 1) * width)
            high_ref[to, columns] = high[of]
            low_ref[to, columns] = low[of]

    for i in range(LAGS + 1):
        if i < LAGS:
            projected = 0.0
            for first, right in sides:
                left = jnp.concatenate([lagged[7 + i - k - first] for k in range(lags)], 1)
                if i == LAGS - 1:
                    last = [lagged[8 + i - k - first, rows - 16 : rows, :] for k in range(lags)]
                    left = jnp.concatenate([left, jnp.concatenate(last, 1)], 0)
                projected += jnp.dot(left, right, preferred_element_type=jnp.float32)
            values = feature(projected, shift)
            value = values[:rows]
            if i == 0:
                start = value
        else:
            last = jnp.where(y == Y - 1, 0.0, values[rows + 15 : rows + 16])
            value = jnp.where(at == rows - 1, last, pltpu.roll(start, rows - 1, 0))
        value = value.T
        if i > 0:
            put((i - 1) // 2 + ((i - 1) % 2) * LAGS, previous - value)
        if i % 2 == 1:
            put(i // 2 + LAGS // 2, value)
        previous = value


def window_of(place, lagged, mine, near, swapped, shift):
    rows, pcs = lagged.shape[1:]
    out = jax.ShapeDtypeStruct((CWD, LAGS * 3 // 2 * rows), jnp.bfloat16)
    return pl.pallas_call(
        window_kernel,
        out_shape=(out, out),
        in_specs=[pl.BlockSpec(memory_space=pltpu.SMEM)] + [pl.BlockSpec(memory_space=pltpu.VMEM)] * 9,
        out_specs=[pl.BlockSpec(memory_space=pltpu.VMEM)] * 2,
        compiler_params=pltpu.CompilerParams(vmem_limit_bytes=VMEM),
        cost_estimate=pl.CostEstimate(flops=1 << 33, bytes_accessed=8 << 20, transcendentals=0),
        name="window",
    )(place, lagged, mine, *near, *swapped, shift)


def products_kernel(wh_ref, wl_ref, fh_ref, fl_ref, own_ref, *code_refs):
    third = fh_ref.shape[0] // 3
    width = own_ref.shape[1]
    for n in range(fh_ref.shape[1] // BLOCK):
        columns = slice(n * BLOCK, (n + 1) * BLOCK)
        terms = []
        for part in range(3):
            span = slice(part * third, (part + 1) * third)
            total = jnp.dot(wh_ref[:, span], fh_ref[span, columns], preferred_element_type=jnp.float32)
            total += jnp.dot(wl_ref[:, span], fh_ref[span, columns], preferred_element_type=jnp.float32)
            total += jnp.dot(wh_ref[:, span], fl_ref[span, columns], preferred_element_type=jnp.float32)
            terms.append(total)
        for which, total in enumerate((terms[0] + terms[1], terms[1] - terms[2])):
            own_ref[which, :, columns] = total[:width]
            for by, ref in enumerate(code_refs, 1):
                ref[which, :, columns] = encode(total[by * width : (by + 1) * width])


def products_of(wh, wl, fh, fl):
    width = fh.shape[1]
    part = CWD // Y
    return pl.pallas_call(
        products_kernel,
        out_shape=[jax.ShapeDtypeStruct((2, part, width), jnp.float32)]
        + [jax.ShapeDtypeStruct((2, part, width), jnp.bfloat16)] * 3,
        in_specs=[pl.BlockSpec(memory_space=pltpu.VMEM)] * 4,
        out_specs=[pl.BlockSpec(memory_space=pltpu.VMEM)] * 4,
        compiler_params=pltpu.CompilerParams(vmem_limit_bytes=VMEM),
        cost_estimate=pl.CostEstimate(flops=1 << 20, bytes_accessed=1 << 20, transcendentals=0),
        name="products",
    )(wh, wl, fh, fl)


def after(values, *others):
    return lax.optimization_barrier((values, others))[0]


def local(snapshots, projection, phase_shift):
    rows, pcs = snapshots.shape
    position = lax.axis_index("tm")
    y, z, c = position // (Z * C), position // C % Z, position % C
    x = lax.axis_index("feat")
    place = jnp.stack([y, z, c, x])

    phased = jnp.swapaxes(snapshots.reshape(rows // LAGS, LAGS, pcs), 0, 1)
    ahead, behind, opposite = (move(phased, lambda y, z, c, by=by: (y, z + by, c)) for by in (1, 3, 2))
    own = [phased, ahead, opposite, behind]
    other = swap(phased)
    octets = jnp.stack([jnp.where(c == 1, piece[:, -1], piece[:, 0]) for piece in own])
    octet = lax.dynamic_index_in_dim(octets, jnp.where(c == 1, (z + 1) % Z, z), 0, keepdims=False)

    octet = after(octet, other)
    others = swap(jnp.stack(own[1:]))

    def outward(core):
        def to(y, z, c):
            gy = y + 1 if c == 1 else y - 1
            return (gy, z, c if core == 0 else 1 - c) if 0 <= gy < Y else None

        return move(octet, to)

    straight, crossed = outward(0), outward(1)
    edge = jnp.where(c == 1, jnp.stack([straight, crossed]), jnp.stack([crossed, straight]))

    width = CWD // Z
    phases = phase_shift[None]
    piece, mine = prepare(place, projection, phases)
    share = share_of(0, after(place, ahead), projection)
    shift = lax.dynamic_slice_in_dim(phase_shift, z * width, width, 0)[None]
    piece = after(piece, other)
    near = [around(piece, by) for by in (1, 3)]
    lagged = lag(place, own, other, after(others, near), edge)
    swapped = [swap(v) for v in after(near, lagged)]
    near = [*near, around(after(piece, near), 2)]

    def feats(first, blocks, share, *others):
        return feats_of(first, blocks, place, after(lagged, *others), share, phases)

    def send(codes):
        return [move(codes[by - 1], lambda y, z, c, by=by: (y + by, z, c)) for by in (1, 3, 2)]

    f0 = feats(0, 2, share, shift)
    share = share_of(1, after(place, f0), projection)
    swapped = [*after(swapped, f0), swap(after(near[2], f0))]
    w = window_of(place, lagged, mine, near, after(swapped, share), shift)
    own0, *codes0 = products_of(*w, *f0)
    sent0 = send(codes0)
    f1 = feats(2, 2, share, own0)
    own1, *codes1 = products_of(*w, *after(f1, own0))
    sent0 = after(sent0, own1)
    sent1 = send(after(codes1, sent0))
    part = width // C

    def finish(chunks):
        total = jnp.concatenate([own + sum(decode(v) for v in sent) for own, sent in chunks], 2)
        low, high = total[:, :part], total[:, part:]
        return jnp.where(c == 1, high, low), swap(jnp.where(c == 1, low, high))

    most = finish(after([(own0, sent0)], own1))
    rest = finish([(own1, sent1)])
    ours, theirs = (jnp.concatenate(v, 2) for v in zip(most, rest))
    whole = jnp.where(c == 1, jnp.concatenate([theirs, ours], 2), jnp.concatenate([ours, theirs], 2))
    steps = rows * Y * Z * C
    return whole[0].T / steps, whole[1].T / (steps - 1)


def solution(mesh):
    in_specs = (P("tm", None), P(None, "feat"), P("feat"))
    out_specs = (P("feat", "tm"), P("feat", "tm"))
    return jax.shard_map(local, mesh=mesh, in_specs=in_specs, out_specs=out_specs, check_vma=False)
```
